32 devices in a mesh: lev: 4 (over y, x), lon: 8 (over z, core).
Axes of the slice: x: 2, y: 2, z: 4, core: 2. Of those that a mesh axis runs over, the one named last changes fastest.
Arguments:
- snapshot: bfloat16 [384, 12, 1024], P('lev', None, 'lon'), may hold values from -6 to 6
- cotangent: bfloat16 [384, 12, 1024], P(None, 'lev', 'lon'), may hold values from -6 to 6
- ocean_mask: int32 [12, 1024], P('lev', 'lon'), may hold values 0 or 1
- kernel: bfloat16 [384, 49], replicated, may hold values from -0.875 to 0.875
- norm_gain: float32 [384], replicated, may hold values from 0.1 to 1.9
- norm_shift: float32 [384], replicated, may hold values from -3 to 3
- weight_in: bfloat16 [384, 1536], replicated, may hold values from -0.3125 to 0.3125
- weight_out: bfloat16 [1536, 384], replicated, may hold values from -0.15625 to 0.15625
Outputs:
- result: bfloat16 [384, 12, 1024], P(None, 'lev', 'lon')
- d_snapshot: bfloat16 [384, 12, 1024], P('lev', None, 'lon')
- kernel_grad: float32 [384, 49], replicated
The draws below stay inside these ranges and needn't reach their ends.
All inputs are finite; a program needn't handle non-finite values. No bound on the sum of `ocean_mask` on one device may be relied on, other than what follows from the above.
Results may differ from the reference program's by a relative error of at most 0.0057.
Values may be sent and summed in bfloat16 or wider, within the bound.
No kernel may reach another device: no remote copies, remote signals or barrier semaphores. Data moves between devices by JAX's collectives and lax.ppermute only.
A program may use at most 64 MiB of HBM per device.

```python
import jax
import jax.numpy as jnp
from jax import lax

C = 384
FF = 1536
TAPS = 7
LAT_DEV = 3
LAT_ALL = 12
LON_ALL = 1024


def set_ends(values, own_key, smallest, top_value):
    shape = values.shape
    place = [jax.random.randint(jax.random.fold_in(own_key, axis), (), 0, shape[axis]) for axis in range(len(shape))]
    values = values.at[tuple(place)].set(smallest)
    longest = shape.index(max(shape))
    place[longest] = (place[longest] + 1) % shape[longest]
    return values.at[tuple(place)].set(top_value)


def levels(key, shape, shards, smallest, top_value):
    loudness, own = 1.0, jax.random.fold_in(key, 6)
    for dim, shards_of in shards:
        steps = jnp.exp(jax.random.uniform(jax.random.fold_in(own, dim), (shards_of,), jnp.float32, smallest / len(shards), top_value / len(shards)))
        loudness = loudness * jnp.repeat(steps, shape[dim] // shards_of).reshape([-1 if axis == dim else 1 for axis in range(len(shape))])
    return loudness


def noise(rng, dims, scale, most, cuts=(), kind=jnp.bfloat16):
    factor_of = levels(rng, dims, cuts, -0.22, 0.18) if cuts else 1.0
    values = jax.random.normal(rng, dims, jnp.float32) * scale * factor_of
    return jnp.minimum(jnp.maximum(values, -most), most).astype(kind)


def setup_inputs(seed: int = 0) -> dict:
    key_of = jax.random.split(jax.random.key(seed), 9)
    return {
        "snapshot": noise(key_of[0], (C, LAT_ALL, LON_ALL), 1.0, 6.0, ((0, 4), (2, 8))),
        "cotangent": noise(key_of[1], (C, LAT_ALL, LON_ALL), 1.0, 6.0, ((1, 4), (2, 8))),
        "ocean_mask": set_ends((jax.random.randint(key_of[2], (LAT_ALL, LON_ALL), 0, 4) < 3).astype(jnp.int32), jax.random.fold_in(key_of[2], 1), 0, 1),
        "kernel": noise(key_of[3], (C, TAPS * TAPS), (TAPS * TAPS) ** -0.5, 0.875),
        "norm_gain": jnp.clip(1.0 + 0.18 * jax.random.normal(key_of[4], (C,), jnp.float32), 0.1, 1.9),
        "norm_shift": noise(key_of[5], (C,), 0.5, 3.0, (), jnp.float32),
        "weight_in": noise(key_of[6], (C, FF), C ** -0.5, 0.3125),
        "weight_out": noise(key_of[7], (FF, C), FF ** -0.5, 0.15625),
    }


epsilon = 1e-06
root_half = 0.7071067811865476
inv_root_tau = 0.3989422804014327

def fold_pad(values):
    reach = TAPS // 2
    latitude = values.shape[1]
    mirrored = values[:, latitude - reach:, :][:, ::-1, ::-1]
    floor_rows = jnp.zeros((values.shape[0], reach, values.shape[2]), values.dtype)
    stacked = jnp.concatenate([floor_rows, values, mirrored], axis=1)
    return jnp.concatenate([stacked[:, :, -reach:], stacked, stacked[:, :, :reach]], axis=2)

def taps(padded, weights, height, width):
    source = padded.astype(jnp.float32)
    total = jnp.zeros((padded.shape[0], height, width), jnp.float32)
    for row_off in range(TAPS):
        for col_off in range(TAPS):
            piece = source[:, row_off:row_off + height, col_off:col_off + width]
            total = total + weights[:, row_off, col_off][:, None, None] * piece
    return total

def kernel_terms(padded, d_conv, height, width):
    source = padded.astype(jnp.float32)
    flat = d_conv.astype(jnp.float32)
    terms = []
    for row_off in range(TAPS):
        for col_off in range(TAPS):
            piece = source[:, row_off:row_off + height, col_off:col_off + width]
            terms.append(lax.optimization_barrier(jnp.sum(flat * piece, axis=(1, 2))))
    return jnp.stack(terms, axis=1).reshape(padded.shape[0], TAPS, TAPS)

def fold_term(fold_rows, weights, width):
    reach = TAPS // 2
    lines = []
    for depth in range(reach):
        total = jnp.zeros((fold_rows.shape[0], width), jnp.float32)
        for source in range(reach - depth):
            for col_off in range(TAPS):
                piece = fold_rows[:, source, col_off:col_off + width].astype(jnp.float32)
                total = total + weights[:, reach + 1 + depth + source, col_off][:, None] * piece
        lines.append(total)
    return jnp.stack(lines[::-1], axis=1)

def gelu_slope(hidden):
    return 0.5 * (1.0 + lax.erf(hidden * root_half)) + hidden * jnp.exp(-0.5 * hidden * hidden) * inv_root_tau

def cell_pass(convolved, residual, incoming, ocean, norm_gain, norm_shift, weight_in, weight_out):
    centre = lax.optimization_barrier(jnp.mean(convolved, axis=0, keepdims=True))
    centred = convolved - centre
    spread = lax.optimization_barrier(jnp.mean(centred * centred, axis=0, keepdims=True))
    rstd = lax.rsqrt(spread + epsilon)
    normed = centred * rstd
    lifted = (normed * norm_gain[:, None] + norm_shift[:, None]).astype(jnp.bfloat16)
    hidden = lax.dot_general(weight_in, lifted, (((0,), (0,)), ((), ())), preferred_element_type=jnp.float32)
    active = jax.nn.gelu(hidden, approximate=False).astype(jnp.bfloat16)
    projected = lax.dot_general(weight_out, active, (((0,), (0,)), ((), ())), preferred_element_type=jnp.float32)
    wet = ocean.astype(jnp.float32)[None, :]
    result = (wet * (residual.astype(jnp.float32) + projected)).astype(jnp.bfloat16)
    upstream = incoming.astype(jnp.float32) * wet
    d_active = jnp.dot(weight_out, upstream.astype(jnp.bfloat16), preferred_element_type=jnp.float32)
    d_hidden = (d_active * gelu_slope(hidden)).astype(jnp.bfloat16)
    d_lifted = jnp.dot(weight_in, d_hidden, preferred_element_type=jnp.float32)
    d_normed = d_lifted * norm_gain[:, None]
    first = lax.optimization_barrier(jnp.mean(d_normed, axis=0, keepdims=True))
    second = lax.optimization_barrier(jnp.mean(d_normed * normed, axis=0, keepdims=True))
    d_conv = (rstd * (d_normed - first - normed * second)).astype(jnp.bfloat16)
    return (result, upstream, d_conv)

def reference(snapshot, cotangent, ocean_mask, kernel, norm_gain, norm_shift, weight_in, weight_out):
    channels, latitude, longitude = snapshot.shape
    reach = TAPS // 2
    weights = kernel.astype(jnp.float32).reshape(channels, TAPS, TAPS)
    flipped = weights[:, ::-1, ::-1]
    padded = fold_pad(snapshot)
    count = LAT_DEV * longitude
    blocks = jnp.arange(latitude // LAT_DEV, dtype=jnp.int32)

    def forward_block(carry, block):
        start = (block * LAT_DEV).astype(jnp.int32)
        window = lax.dynamic_slice_in_dim(padded, start, LAT_DEV + 2 * reach, 1)
        convolved = taps(window, weights, LAT_DEV, longitude)
        residual = window[:, reach:reach + LAT_DEV, reach:reach + longitude]
        incoming = lax.dynamic_slice_in_dim(cotangent, start, LAT_DEV, 1)
        ocean = lax.dynamic_slice_in_dim(ocean_mask, start, LAT_DEV, 0)
        result, upstream, d_conv = cell_pass(convolved.reshape(channels, count), residual.reshape(channels, count), incoming.reshape(channels, count), ocean.reshape(count), norm_gain, norm_shift, weight_in, weight_out)
        d_conv = d_conv.reshape(channels, LAT_DEV, longitude)
        carry = carry + kernel_terms(window, d_conv, LAT_DEV, longitude)
        return (carry, (result.reshape(channels, LAT_DEV, longitude), upstream.reshape(channels, LAT_DEV, longitude), d_conv))
    kernel_grad, (results, upstreams, d_convs) = lax.scan(forward_block, jnp.zeros((channels, TAPS, TAPS), jnp.float32), blocks)

    def join(stack):
        return jnp.moveaxis(stack, 0, 1).reshape(channels, latitude, longitude)
    result = join(results)
    upstream = join(upstreams)
    d_conv = join(d_convs)
    d_padded = fold_pad(d_conv)
    fold_rows = d_padded[:, latitude + reach:, :]
    regular = jnp.concatenate([d_padded[:, :latitude + reach], jnp.zeros_like(fold_rows)], axis=1)

    def adjoint_block(block):
        start = (block * LAT_DEV).astype(jnp.int32)
        window = lax.dynamic_slice_in_dim(regular, start, LAT_DEV + 2 * reach, 1)
        return taps(window, flipped, LAT_DEV, longitude)
    adjoint = join(lax.map(adjoint_block, blocks))
    edge = fold_term(fold_rows, weights, longitude)
    adjoint = adjoint.at[:, latitude - reach:, :].add(edge)
    d_snapshot = (upstream + adjoint).astype(jnp.bfloat16)
    return (result, d_snapshot, kernel_grad.reshape(channels, TAPS * TAPS))
```

```python
import jax
import jax.numpy as jnp
from jax import lax
from jax.experimental import pallas as pl
from jax.experimental.pallas import tpu as pltpu
from jax.sharding import PartitionSpec as P

TAPS = 7
REACH = TAPS // 2
EPSILON = 1e-06
ROOT_HALF = 0.7071067811865476
INV_ROOT_TAU = 0.3989422804014327
F32 = jnp.float32
BF16 = jnp.bfloat16
VMEM = pl.BlockSpec(memory_space=pltpu.VMEM)
SMEM = pl.BlockSpec(memory_space=pltpu.SMEM)
SPAN = 2 * REACH
LIMIT = 48 * 1024 * 1024


def call(body, out, specs, scratch, flops, moved, name):
    return pl.pallas_call(
        body,
        out_shape=out,
        in_specs=specs,
        out_specs=jax.tree.map(lambda _: VMEM, out),
        scratch_shapes=scratch,
        compiler_params=pltpu.CompilerParams(vmem_limit_bytes=LIMIT),
        cost_estimate=pl.CostEstimate(flops=flops, bytes_accessed=moved, transcendentals=0),
        name=name,
    )


def shaped(*shape, dtype=BF16):
    return jax.ShapeDtypeStruct(shape, dtype)


def lanes_of(shape):
    return lax.broadcasted_iota(jnp.int32, shape, len(shape) - 1)


def groups_of(rows):
    per = rows
    while per * SPAN > 128 or rows % per:
        per -= 1
    return rows // per, per


def pack_edges(read, odd, off_ref, on_ref, rows, channels, width):
    count, per = groups_of(rows)
    lane = lanes_of((channels, width))
    for group in range(count):
        off = jnp.zeros((channels, width), F32)
        on = jnp.zeros((channels, width), F32)
        for place in range(per):
            line = read(group * per + place)
            base = SPAN * place
            first = pltpu.roll(line, base % width, 1)
            last = pltpu.roll(line, base % width, 1)
            in_first = (lane >= base) & (lane < base + REACH)
            spot = (base - REACH) % width
            in_last = (lane >= spot) & (lane < spot + REACH)
            far = jnp.where(odd == 1, in_last.astype(jnp.int32), in_first.astype(jnp.int32))
            near = jnp.where(odd == 1, in_first.astype(jnp.int32), in_last.astype(jnp.int32))
            off = jnp.where(far == 1, first, off)
            on = jnp.where(near == 1, last, on)
        off_ref[group] = off.astype(BF16)
        on_ref[group] = on.astype(BF16)


def near_edges(off, on, odd, lane, width):
    right = ((lane % SPAN < REACH) & (lane < width - REACH)).astype(jnp.int32)
    use_on = jnp.where(odd == 1, 1 - right, right)
    return jnp.where(use_on == 1, on, off)


def flip_lanes(value, width):
    row = lax.broadcasted_iota(jnp.int32, (width, width), 0)
    col = lax.broadcasted_iota(jnp.int32, (width, width), 1)
    exchange = (row + col == width - 1).astype(BF16)
    return jnp.dot(value, exchange, preferred_element_type=F32)


def fill(lines, edges, read, off_ref, on_ref, top_ref, mate_ref, top_off_ref, odd, rows, channels, width):
    count, per = groups_of(rows)
    lane = lanes_of((channels, width))
    for group in range(count):
        mixed = near_edges(off_ref[group].astype(F32), on_ref[group].astype(F32), odd, lane, width)
        for place in range(per):
            row = group * per + place
            lines[row] = read(row)
            edges[row] = pltpu.roll(mixed, (width - SPAN * place) % width, 1)
    for depth in range(REACH):
        row = rows - 1 - depth
        group, place = row // per, row % per
        far = pltpu.roll(top_off_ref[group].astype(F32), (width - SPAN * place) % width, 1)
        near = mate_ref[REACH - 1 - depth].astype(F32)
        right = (lane < width // 2).astype(jnp.int32)
        use_near = jnp.where(odd == 1, right, 1 - right)
        edge = jnp.where(use_near == 1, near, far)
        lines[rows + depth] = flip_lanes(top_ref[REACH - 1 - depth], width)
        edges[rows + depth] = flip_lanes(edge.astype(BF16), width)


def shifted(line, edge, step, lane, width):
    if step == 0:
        return line
    if step > 0:
        return pltpu.roll(jnp.where(lane < step, edge, line), width - step, 1)
    return pltpu.roll(jnp.where(lane >= width + step, edge, line), -step, 1)


def prepare_body(levels, channels, rows, width):
    height = rows // levels

    def body(place_ref, snap_ref, off_ref, on_ref, top_ref, *rest):
        sends, lines = rest[:levels], rest[levels]
        lev, odd = place_ref[0], place_ref[1]
        lines[...] = jnp.swapaxes(snap_ref[...].astype(F32), 0, 1)
        for hop in range(levels):
            start = (lev ^ hop) * height
            sends[hop][...] = lines[pl.ds(start, height)].astype(BF16)
        top_ref[...] = lines[rows - REACH :].astype(BF16)
        pack_edges(lambda row: lines[row], odd, off_ref, on_ref, rows, channels, width)

    return body


def conv_body(levels, channels, rows, width):
    height = rows // levels

    def body(place_ref, snap_ref, off_ref, on_ref, top_ref, mate_ref, top_off_ref, weight_ref, *rest):
        sends, (lines, edges, total) = rest[:levels], rest[levels:]
        lev, odd = place_ref[0], place_ref[1]
        total[...] = jnp.swapaxes(snap_ref[...].astype(F32), 0, 1)
        fill(lines, edges, lambda row: total[row], off_ref, on_ref, top_ref, mate_ref, top_off_ref, odd, rows, channels, width)
        lane = lanes_of((8, width))

        def step(block, carry):
            span = pl.ds(block * 8, 8)
            weights = weight_ref[span, :]
            sums = [None] * rows
            for col in range(TAPS):
                taps = [jnp.broadcast_to(weights[:, a * TAPS + col : a * TAPS + col + 1], (8, width)) for a in range(TAPS)]
                for source in range(rows + REACH):
                    moved = shifted(lines[source, span, :], edges[source, span, :], col - REACH, lane, width)
                    for a in range(TAPS):
                        row = source - a + REACH
                        if 0 <= row < rows:
                            term = taps[a] * moved
                            sums[row] = term if sums[row] is None else sums[row] + term
            for row in range(rows):
                total[row, span, :] = sums[row]
            return carry

        lax.fori_loop(0, channels // 8, step, 0)
        for hop in range(levels):
            sends[hop][...] = total[pl.ds((lev ^ hop) * height, height)].astype(BF16)

    return body


def cotangent_body(levels, channels, height, width):
    def body(place_ref, cot_ref, mask_ref, up_ref, *rest):
        sends, lines = rest[:levels], rest[levels]
        lev = place_ref[0]
        wet = mask_ref[...].astype(F32)
        lines[...] = jnp.swapaxes(cot_ref[...].astype(F32), 0, 1) * wet[:, None, :]
        for row in range(height):
            up_ref[:, row * width : (row + 1) * width] = lines[row].astype(BF16)
        for hop in range(levels):
            start = pl.multiple_of((lev ^ hop) * channels, 8)
            for row in range(height):
                sends[hop][row] = lines[row, pl.ds(start, channels), :].astype(BF16)

    return body


def cell_body(levels, channels, height, width, chunk):
    total_channels = levels * channels
    cells = height * width

    def body(place_ref, *refs):
        convs, snaps, refs = refs[:levels], refs[levels : 2 * levels], refs[2 * levels :]
        up_ref, mask_ref, gain_ref, shift_ref, win_ref, wint_ref, wout_ref, woutt_ref = refs[:8]
        result_ref, sends = refs[8], refs[9 : 9 + levels]
        field, d_lifted, projected = refs[9 + levels :]
        lev = place_ref[0]
        for hop in range(levels):
            start = pl.multiple_of((lev ^ hop) * channels, 8)
            for row in range(height):
                field[pl.ds(start, channels), row * width : (row + 1) * width] = convs[hop][row].astype(F32)
        convolved = field[...]
        centre = jnp.mean(convolved, axis=0, keepdims=True)
        centred = convolved - centre
        spread = jnp.mean(centred * centred, axis=0, keepdims=True)
        rstd = lax.rsqrt(spread + EPSILON)
        normed = centred * rstd
        field[...] = normed
        gain = gain_ref[...]
        lifted = (normed * gain + shift_ref[...]).astype(BF16)
        upstream = up_ref[...]
        features = wout_ref.shape[0]
        for piece in range(features // chunk):
            span = slice(piece * chunk, (piece + 1) * chunk)
            hidden = jnp.dot(wint_ref[span, :], lifted, preferred_element_type=F32)
            d_active = jnp.dot(wout_ref[span, :], upstream, preferred_element_type=F32)
            half = 0.5 * (1.0 + lax.erf(hidden * ROOT_HALF))
            active = (hidden * half).astype(BF16)
            slope = half + hidden * jnp.exp(-0.5 * hidden * hidden) * INV_ROOT_TAU
            d_hidden = (d_active * slope).astype(BF16)
            out = jnp.dot(woutt_ref[:, span], active, preferred_element_type=F32)
            back = jnp.dot(win_ref[:, span], d_hidden, preferred_element_type=F32)
            if piece == 0:
                projected[...] = out
                d_lifted[...] = back
            else:
                projected[...] += out
                d_lifted[...] += back
        for hop in range(levels):
            start = pl.multiple_of((lev ^ hop) * channels, 8)
            for row in range(height):
                wet = mask_ref[row : row + 1, :].astype(F32)
                value = snaps[hop][row].astype(F32) + projected[pl.ds(start, channels), row * width : (row + 1) * width]
                projected[pl.ds(start, channels), row * width : (row + 1) * width] = wet * value
        for row in range(height):
            result_ref[row] = projected[:, row * width : (row + 1) * width].astype(BF16)
        d_normed = d_lifted[...] * gain
        normed = field[...]
        first = jnp.mean(d_normed, axis=0, keepdims=True)
        second = jnp.mean(d_normed * normed, axis=0, keepdims=True)
        field[...] = rstd * (d_normed - first - normed * second)
        for hop in range(levels):
            start = pl.multiple_of((lev ^ hop) * channels, 8)
            for row in range(height):
                sends[hop][row] = field[pl.ds(start, channels), row * width : (row + 1) * width].astype(BF16)

    return body


def gather_body(levels, channels, rows, width):
    height = rows // levels

    def body(place_ref, *refs):
        blocks, (lines_ref, off_ref, on_ref, top_ref, lines) = refs[:levels], refs[levels:]
        lev, odd = place_ref[0], place_ref[1]
        for hop in range(levels):
            lines[pl.ds((lev ^ hop) * height, height)] = blocks[hop][...].astype(F32)
        lines_ref[...] = lines[...].astype(BF16)
        top_ref[...] = lines[rows - REACH :].astype(BF16)
        pack_edges(lambda row: lines[row], odd, off_ref, on_ref, rows, channels, width)

    return body


def kernel_body(channels, rows, width):
    def body(place_ref, snap_ref, off_ref, on_ref, top_ref, mate_ref, top_off_ref, d_ref, out_ref, lines, edges, source_lines, d_lines):
        odd = place_ref[1]
        source_lines[...] = jnp.swapaxes(snap_ref[...].astype(F32), 0, 1)
        d_lines[...] = d_ref[...].astype(F32)
        fill(lines, edges, lambda row: source_lines[row], off_ref, on_ref, top_ref, mate_ref, top_off_ref, odd, rows, channels, width)
        lane = lanes_of((8, width))
        out_lane = lanes_of((8, 128))

        def step(block, carry):
            span = pl.ds(block * 8, 8)
            grad = [d_lines[row, span, :] for row in range(rows)]
            found = jnp.zeros((8, 128), F32)
            for col in range(TAPS):
                sums = [None] * TAPS
                for source in range(rows + REACH):
                    moved = shifted(lines[source, span, :], edges[source, span, :], col - REACH, lane, width)
                    for a in range(TAPS):
                        row = source - a + REACH
                        if 0 <= row < rows:
                            term = grad[row] * moved
                            sums[a] = term if sums[a] is None else sums[a] + term
                for a in range(TAPS):
                    found = jnp.where(out_lane == a * TAPS + col, jnp.sum(sums[a], axis=1, keepdims=True), found)
            out_ref[span, :] = found
            return carry

        lax.fori_loop(0, channels // 8, step, 0)

    return body


def adjoint_body(levels, channels, rows, width):
    height = rows // levels

    def body(place_ref, d_ref, off_ref, on_ref, top_ref, mate_ref, top_off_ref, weight_ref, *refs):
        ups, (out_ref, lines, edges, total) = refs[:levels], refs[levels:]
        lev, odd = place_ref[0], place_ref[1]
        fill(lines, edges, lambda row: d_ref[row].astype(F32), off_ref, on_ref, top_ref, mate_ref, top_off_ref, odd, rows, channels, width)
        for hop in range(levels):
            total[pl.ds((lev ^ hop) * height, height)] = ups[hop][...].astype(F32)
        lane = lanes_of((8, width))

        def step(block, carry):
            span = pl.ds(block * 8, 8)
            weights = weight_ref[span, :]
            sums = [None] * rows
            for col in range(TAPS):
                taps = [jnp.broadcast_to(weights[:, a * TAPS + col : a * TAPS + col + 1], (8, width)) for a in range(TAPS)]
                for source in range(rows):
                    moved = shifted(lines[source, span, :], edges[source, span, :], REACH - col, lane, width)
                    for a in range(TAPS):
                        row = source + a - REACH
                        if 0 <= row < rows:
                            term = taps[a] * moved
                            sums[row] = term if sums[row] is None else sums[row] + term
                for source in range(REACH):
                    moved = shifted(lines[rows + source, span, :], edges[rows + source, span, :], col - REACH, lane, width)
                    for depth in range(REACH - source):
                        row = rows - 1 - depth
                        sums[row] = sums[row] + taps[REACH + 1 + depth + source] * moved
            for row in range(rows):
                total[row, span, :] = total[row, span, :] + sums[row]
            return carry

        lax.fori_loop(0, channels // 8, step, 0)
        out_ref[...] = jnp.swapaxes(total[...], 0, 1).astype(BF16)

    return body


def across(value, axis, target):
    count = lax.axis_size(axis)
    return lax.ppermute(value, axis, [(i, target(i) % count) for i in range(count)])


def level_swap(blocks):
    return [blocks[0]] + [across(blocks[hop], "lev", lambda i: i ^ hop) for hop in range(1, len(blocks))]


def edge_swap(off, on, top):
    lanes = lax.axis_size("lon")
    near = across(on, "lon", lambda i: i ^ 1)
    far = across(off, "lon", lambda i: i + 1 if i % 2 else i - 1)
    folded = across(top, "lon", lambda i: lanes - 1 - i)
    fold_far = across(off, "lon", lambda i: lanes - 2 - i if i % 2 else lanes - i)
    mate = across(folded, "lon", lambda i: i ^ 1)
    return far, near, folded, mate, fold_far


def shards(snapshot, cotangent, ocean_mask, kernel, norm_gain, norm_shift, weight_in, weight_out):
    levels = lax.axis_size("lev")
    lanes = lax.axis_size("lon")
    channels, rows, width = snapshot.shape
    height = rows // levels
    total_channels = channels * levels
    features = weight_in.shape[1]
    cells = height * width
    lev = lax.axis_index("lev")
    place = jnp.stack([lev, lax.axis_index("lon") % 2]).astype(jnp.int32)
    groups = groups_of(rows)[0]
    weights = lax.dynamic_slice_in_dim(kernel, lev * channels, channels, 0).astype(F32)
    weights = jnp.pad(weights, ((0, 0), (0, 128 - TAPS * TAPS)))
    block = shaped(height, channels, width)
    pack = shaped(groups, channels, width)
    top_shape = shaped(REACH, channels, width)
    field = pltpu.VMEM((rows, channels, width), F32)
    deep = pltpu.VMEM((rows + REACH, channels, width), F32)
    moved = channels * rows * width * 2

    off, on, top, *snap_sends = call(
        prepare_body(levels, channels, rows, width),
        [pack, pack, top_shape] + [block] * levels,
        [SMEM, VMEM],
        [field],
        moved,
        2 * moved,
        "prepare",
    )(place, snapshot)
    snap_edges = edge_swap(off, on, top)
    snaps = level_swap(snap_sends)
    upstream, *up_sends = call(
        cotangent_body(levels, channels, height, width),
        [shaped(total_channels, cells)] + [block] * levels,
        [SMEM, VMEM, VMEM],
        [pltpu.VMEM((height, total_channels, width), F32)],
        moved,
        2 * moved,
        "cotangent",
    )(place, cotangent, ocean_mask)
    ups = level_swap(up_sends)
    conv_sends = call(
        conv_body(levels, channels, rows, width),
        [block] * levels,
        [SMEM] + [VMEM] * 7,
        [deep, deep, field],
        98 * moved,
        2 * moved,
        "depthwise",
    )(place, snapshot, *snap_edges, weights)
    convs = level_swap(conv_sends)
    cell_fields = [pltpu.VMEM((total_channels, cells), F32)] * 3
    result, *d_sends = call(
        cell_body(levels, channels, height, width, 256),
        [shaped(height, total_channels, width)] + [block] * levels,
        [SMEM] + [VMEM] * (2 * levels + 8),
        cell_fields,
        8 * total_channels * features * cells,
        10 * moved,
        "cells",
    )(
        place,
        *convs,
        *snaps,
        upstream,
        ocean_mask,
        norm_gain[:, None],
        norm_shift[:, None],
        weight_in,
        weight_in.T,
        weight_out,
        weight_out.T,
    )
    d_blocks = level_swap(d_sends)
    d_lines, off, on, top = call(
        gather_body(levels, channels, rows, width),
        [shaped(rows, channels, width), pack, pack, top_shape],
        [SMEM] + [VMEM] * levels,
        [field],
        moved,
        2 * moved,
        "regroup",
    )(place, *d_blocks)
    d_edges = edge_swap(off, on, top)
    terms = call(
        kernel_body(channels, rows, width),
        shaped(channels, 128, dtype=F32),
        [SMEM] + [VMEM] * 7,
        [deep, deep, field, field],
        98 * moved,
        2 * moved,
        "kernel_terms",
    )(place, snapshot, *snap_edges, d_lines)
    hop = 1
    while hop < lanes:
        terms = terms + across(terms, "lon", lambda i: i ^ hop)
        hop *= 2
    parts = level_swap([terms] * levels)
    stacked = jnp.zeros((levels, channels, 128), F32)
    for hop, part in enumerate(parts):
        stacked = lax.dynamic_update_slice(stacked, part[None], (lev ^ hop, 0, 0))
    kernel_grad = stacked.reshape(total_channels, 128)[:, : TAPS * TAPS]
    d_snapshot = call(
        adjoint_body(levels, channels, rows, width),
        shaped(channels, rows, width),
        [SMEM] + [VMEM] * (7 + levels),
        [deep, deep, field],
        98 * moved,
        2 * moved,
        "adjoint",
    )(place, d_lines, *d_edges, weights, *ups)
    return (jnp.swapaxes(result, 0, 1), d_snapshot, kernel_grad)


def solution(mesh):
    placed = (
        P("lev", None, "lon"),
        P(None, "lev", "lon"),
        P("lev", "lon"),
        P(),
        P(),
        P(),
        P(),
        P(),
    )
    return jax.shard_map(
        shards,
        mesh=mesh,
        in_specs=placed,
        out_specs=(P(None, "lev", "lon"), P("lev", None, "lon"), P()),
        check_vma=False,
    )
```

```python
import jax
import jax.numpy as jnp
from jax import lax
from jax.experimental import pallas as pl
from jax.experimental.pallas import tpu as pltpu
from jax.sharding import PartitionSpec as P

TAPS = 7
REACH = TAPS // 2
EPSILON = 1e-06
ROOT_HALF = 0.7071067811865476
INV_ROOT_TAU = 0.3989422804014327
F32 = jnp.float32
BF16 = jnp.bfloat16
VMEM = pl.BlockSpec(memory_space=pltpu.VMEM)
SMEM = pl.BlockSpec(memory_space=pltpu.SMEM)
SPAN = 2 * REACH
FIRST = (((0,), (0,)), ((), ()))
LIMIT = 24 * 1024 * 1024


def call(body, out, specs, scratch, micros, name):
    return pl.pallas_call(
        body,
        out_shape=out,
        in_specs=specs,
        out_specs=jax.tree.map(lambda _: VMEM, out),
        scratch_shapes=scratch,
        compiler_params=pltpu.CompilerParams(vmem_limit_bytes=LIMIT),
        cost_estimate=pl.CostEstimate(flops=int(micros * 1.1e9), bytes_accessed=0, transcendentals=0),
        name=name,
    )


def shaped(*shape, dtype=BF16):
    return jax.ShapeDtypeStruct(shape, dtype)


def lanes_of(shape):
    return lax.broadcasted_iota(jnp.int32, shape, len(shape) - 1)


def groups_of(rows):
    per = rows
    while (per + 2 * REACH) * SPAN > 128 or rows % per:
        per -= 1
    return rows // per, per


def where_flag(flag, yes, no):
    return jnp.where(flag == 1, yes.astype(jnp.int32), no.astype(jnp.int32)) == 1


def right_lanes(lane, per, width):
    low = (per + REACH) * SPAN - REACH
    base = SPAN * ((width + SPAN - 1) // SPAN) - width
    return jnp.where(lane >= low, lane + base, lane) % SPAN < REACH


def pack_edges(read, odd, off_ref, on_ref, rows, channels, width):
    count, per = groups_of(rows)
    lane = lanes_of((channels, width))
    for group in range(count):
        off = jnp.zeros((channels, width), F32)
        on = jnp.zeros((channels, width), F32)
        for place in range(per):
            base = SPAN * place
            line = pltpu.roll(read(group * per + place), base, 1) if place else read(group * per)
            in_first = (lane >= base) & (lane < base + REACH)
            spot = (base - REACH) % width
            in_last = (lane >= spot) & (lane < spot + REACH)
            off = jnp.where(where_flag(odd, in_last, in_first), line, off)
            on = jnp.where(where_flag(odd, in_first, in_last), line, on)
        off_ref[group] = off.astype(BF16)
        on_ref[group] = on.astype(BF16)


def flip_lanes(value, width, top):
    row = lax.broadcasted_iota(jnp.int32, (width, width), 0)
    col = lax.broadcasted_iota(jnp.int32, (width, width), 1)
    exchange = ((row + col) % width == top % width).astype(BF16)
    return jnp.dot(value, exchange, preferred_element_type=F32)


def packed_edges(off_ref, on_ref, top_ref, mate_ref, fold_ref, odd, rows, channels, width):
    count, per = groups_of(rows)
    lane = lanes_of((channels, width))
    right = right_lanes(lane, per, width)
    near = where_flag(odd, ~right, right)
    groups = [jnp.where(near, on_ref[g].astype(F32), off_ref[g].astype(F32)) for g in range(count)]
    fold = jnp.where(near, fold_ref[count - 1].astype(F32), 0.0)
    ends = SPAN * (per - REACH) - REACH
    fold = jnp.where((lane >= ends) & (lane < SPAN * per - REACH), fold, 0.0)
    for depth in range(REACH):
        base = SPAN * (per - 1 - depth)
        line = pltpu.roll(mate_ref[REACH - 1 - depth].astype(F32), base, 1)
        here = (lane >= base - REACH) & (lane < base + REACH) & ~near
        fold = jnp.where(here, line, fold)
    groups[-1] = groups[-1] + flip_lanes(fold.astype(BF16), width, 2 * SPAN * per - SPAN - 1)
    return groups


def unpack(group, place, width):
    shift = (-SPAN * place) % width
    return pltpu.roll(group, shift, 1) if shift else group


def fill(lines, edges, read, off_ref, on_ref, top_ref, mate_ref, fold_ref, odd, rows, channels, width):
    count, per = groups_of(rows)
    groups = packed_edges(off_ref, on_ref, top_ref, mate_ref, fold_ref, odd, rows, channels, width)
    for row in range(rows):
        lines[row] = read(row)
        edges[row] = unpack(groups[row // per], row % per, width)
    for depth in range(REACH):
        lines[rows + depth] = flip_lanes(top_ref[REACH - 1 - depth], width, width - 1)
        edges[rows + depth] = unpack(groups[-1], per + depth, width)


def shifted(line, edge, step, lane, width):
    if step == 0:
        return line
    if step > 0:
        return pltpu.roll(jnp.where(lane < step, edge, line), width - step, 1)
    return pltpu.roll(jnp.where(lane >= width + step, edge, line), -step, 1)


def prepare_body(levels, channels, rows, width):
    height = rows // levels

    def body(place_ref, snap_ref, off_ref, on_ref, top_ref, *sends):
        lev, odd = place_ref[0], place_ref[1]
        pack_edges(lambda row: snap_ref[row].astype(F32), odd, off_ref, on_ref, rows, channels, width)
        top_ref[...] = snap_ref[rows - REACH :]
        for hop in range(1, levels):
            sends[hop - 1][...] = snap_ref[pl.ds((lev ^ hop) * height, height)]

    return body


def inner_body(channels, rows, width):
    def body(snap_ref, weight_ref, out_ref, spread_ref, lines):
        lines[...] = snap_ref[...].astype(F32)
        lane = lanes_of((8, width))

        def step(block, carry):
            span = pl.ds(block * 8, 8)
            weights = weight_ref[span, :]
            sums = [None] * rows
            for col in range(TAPS):
                taps = [jnp.broadcast_to(weights[:, a * TAPS + col : a * TAPS + col + 1], (8, width)) for a in range(TAPS)]
                for a in range(TAPS):
                    spread_ref[a * TAPS + col, span, :] = taps[a]
                for source in range(rows):
                    moved = shifted(lines[source, span, :], 0.0, col - REACH, lane, width)
                    for a in range(TAPS):
                        row = source - a + REACH
                        if 0 <= row < rows:
                            term = taps[a] * moved
                            sums[row] = term if sums[row] is None else sums[row] + term
            for row in range(rows):
                out_ref[row, span, :] = sums[row]
            return carry

        lax.fori_loop(0, channels // 8, step, 0)

    return body


def outer_body(levels, channels, rows, width):
    height = rows // levels
    count, per = groups_of(rows)

    def body(place_ref, inner_ref, off_ref, on_ref, top_ref, mate_ref, fold_ref, spread_ref, *rest):
        sends, (total, packed, folded) = rest[:levels], rest[levels:]
        lev, odd = place_ref[0], place_ref[1]
        groups = packed_edges(off_ref, on_ref, top_ref, mate_ref, fold_ref, odd, rows, channels, width)
        wide = lanes_of((channels, width))
        for group in range(count):
            value = groups[group]
            if group:
                tail = (wide >= SPAN * (per - REACH) - REACH) & (wide < SPAN * per - REACH)
                value = value + pltpu.roll(jnp.where(tail, groups[group - 1], 0.0), (-SPAN * per) % width, 1)
            if group + 1 < count:
                begin = (wide < SPAN * REACH - REACH) | (wide >= width - REACH)
                value = value + pltpu.roll(jnp.where(begin, groups[group + 1], 0.0), SPAN * per, 1)
            packed[group] = value
        for depth in range(REACH):
            folded[depth] = flip_lanes(top_ref[REACH - 1 - depth], width, width - 1)
        lane = lanes_of((8, width))
        right = right_lanes(lane, per, width)
        rim = (lane < REACH) | (lane >= width - REACH)

        def step(block, carry):
            span = pl.ds(block * 8, 8)
            for group in range(count):
                near = packed[group, span, :]
                from_right = jnp.where(right, near, 0.0)
                from_left = jnp.where(right, 0.0, near)
                sums = [None, None]
                for a in range(TAPS):
                    for col in range(TAPS):
                        if col == REACH:
                            continue
                        side = col > REACH
                        move = (-(SPAN * (a - REACH) + col - REACH)) % width
                        term = spread_ref[a * TAPS + col, span, :] * pltpu.roll(from_right if side else from_left, move, 1)
                        sums[side] = term if sums[side] is None else sums[side] + term
                rims = jnp.where(right, sums[0], sums[1])
                for place in range(per):
                    row = group * per + place
                    value = inner_ref[row, span, :] + jnp.where(rim, unpack(rims, place, width), 0.0)
                    if row >= rows - REACH:
                        for depth in range(REACH):
                            a = rows + depth - row + REACH
                            if a < TAPS:
                                for col in range(TAPS):
                                    moved = shifted(folded[depth, span, :], 0.0, col - REACH, lane, width)
                                    value = value + spread_ref[a * TAPS + col, span, :] * moved
                    total[row, span, :] = value
            return carry

        lax.fori_loop(0, channels // 8, step, 0)
        for hop in range(levels):
            sends[hop][...] = total[pl.ds((lev ^ hop) * height, height)].astype(BF16)

    return body


def columns_body(channels, rows, width):
    def body(place_ref, snap_ref, off_ref, on_ref, top_ref, mate_ref, fold_ref, out_ref, lines, edges):
        odd = place_ref[1]
        fill(lines, edges, lambda row: snap_ref[row].astype(F32), off_ref, on_ref, top_ref, mate_ref, fold_ref, odd, rows, channels, width)
        lane = lanes_of((channels, width))
        for col in range(TAPS):
            for source in range(rows + REACH):
                out_ref[col, source] = shifted(lines[source], edges[source], col - REACH, lane, width)

    return body


def cotangent_body(levels, channels, height, width):
    def body(place_ref, cot_ref, mask_ref, up_ref, *rest):
        sends, lines = rest[:levels], rest[levels]
        lev = place_ref[0]
        wet = mask_ref[...].astype(F32)
        lines[...] = cot_ref[...].astype(F32) * wet[:, None, :]
        for row in range(height):
            up_ref[:, row * width : (row + 1) * width] = lines[row].astype(BF16)
        for hop in range(levels):
            start = pl.multiple_of((lev ^ hop) * channels, 8)
            for row in range(height):
                sends[hop][row] = lines[row, pl.ds(start, channels), :].astype(BF16)

    return body


def cell_body(levels, channels, height, width, chunk):
    total_channels = levels * channels
    cells = height * width

    def body(place_ref, *refs):
        convs, snaps, own_ref, refs = refs[:levels], refs[levels : 2 * levels - 1], refs[2 * levels - 1], refs[2 * levels :]
        up_ref, mask_ref, gain_ref, shift_ref, win_ref, wout_ref = refs[:6]
        result_ref, sends = refs[6], refs[7 : 7 + levels]
        field, d_lifted, projected = refs[7 + levels :]
        lev = place_ref[0]
        for hop in range(levels):
            start = pl.multiple_of((lev ^ hop) * channels, 8)
            for row in range(height):
                field[pl.ds(start, channels), row * width : (row + 1) * width] = convs[hop][row].astype(F32)
        convolved = field[...]
        centre = jnp.mean(convolved, axis=0, keepdims=True)
        centred = convolved - centre
        spread = jnp.mean(centred * centred, axis=0, keepdims=True)
        rstd = lax.rsqrt(spread + EPSILON)
        normed = centred * rstd
        field[...] = normed
        gain = gain_ref[...]
        lifted = (normed * gain + shift_ref[...]).astype(BF16)
        upstream = up_ref[...]
        features = wout_ref.shape[0]
        for piece in range(features // chunk):
            span = slice(piece * chunk, (piece + 1) * chunk)
            hidden = lax.dot_general(win_ref[:, span], lifted, FIRST, preferred_element_type=F32)
            d_active = jnp.dot(wout_ref[span, :], upstream, preferred_element_type=F32)
            half = 0.5 * (1.0 + lax.erf(hidden * ROOT_HALF))
            active = (hidden * half).astype(BF16)
            slope = half + hidden * jnp.exp(-0.5 * hidden * hidden) * INV_ROOT_TAU
            d_hidden = (d_active * slope).astype(BF16)
            out = lax.dot_general(wout_ref[span, :], active, FIRST, preferred_element_type=F32)
            back = jnp.dot(win_ref[:, span], d_hidden, preferred_element_type=F32)
            if piece == 0:
                projected[...] = out
                d_lifted[...] = back
            else:
                projected[...] += out
                d_lifted[...] += back
        for hop in range(levels):
            start = pl.multiple_of((lev ^ hop) * channels, 8)
            for row in range(height):
                wet = mask_ref[row : row + 1, :].astype(F32)
                held = snaps[hop - 1][row] if hop else own_ref[lev * height + row]
                value = held.astype(F32) + projected[pl.ds(start, channels), row * width : (row + 1) * width]
                projected[pl.ds(start, channels), row * width : (row + 1) * width] = wet * value
        for row in range(height):
            result_ref[row] = projected[:, row * width : (row + 1) * width].astype(BF16)
        d_normed = d_lifted[...] * gain
        normed = field[...]
        first = jnp.mean(d_normed, axis=0, keepdims=True)
        second = jnp.mean(d_normed * normed, axis=0, keepdims=True)
        field[...] = rstd * (d_normed - first - normed * second)
        for hop in range(levels):
            start = pl.multiple_of((lev ^ hop) * channels, 8)
            for row in range(height):
                sends[hop][row] = field[pl.ds(start, channels), row * width : (row + 1) * width].astype(BF16)

    return body


def gather_body(levels, channels, rows, width):
    height = rows // levels

    def body(place_ref, *refs):
        blocks, (lines_ref, off_ref, on_ref, top_ref, lines) = refs[:levels], refs[levels:]
        lev, odd = place_ref[0], place_ref[1]
        for hop in range(levels):
            lines[pl.ds((lev ^ hop) * height, height)] = blocks[hop][...].astype(F32)
        lines_ref[...] = lines[...].astype(BF16)
        top_ref[...] = lines[rows - REACH :].astype(BF16)
        pack_edges(lambda row: lines[row], odd, off_ref, on_ref, rows, channels, width)

    return body


def kernel_body(levels, channels, rows, width):
    height = rows // levels

    def body(place_ref, columns_ref, *refs):
        blocks, (out_ref, grads) = refs[:levels], refs[levels:]
        lev = place_ref[0]
        for hop in range(levels):
            grads[pl.ds((lev ^ hop) * height, height)] = blocks[hop][...].astype(F32)
        out_lane = lanes_of((8, 128))

        def step(block, carry):
            span = pl.ds(block * 8, 8)
            grad = [grads[row, span, :] for row in range(rows)]
            found = jnp.zeros((8, 128), F32)
            for col in range(TAPS):
                sums = [None] * TAPS
                for source in range(rows + REACH):
                    moved = columns_ref[col, source, span, :]
                    for a in range(TAPS):
                        row = source - a + REACH
                        if 0 <= row < rows:
                            term = grad[row] * moved
                            sums[a] = term if sums[a] is None else sums[a] + term
                for a in range(TAPS):
                    found = jnp.where(out_lane == a * TAPS + col, jnp.sum(sums[a], axis=1, keepdims=True), found)
            out_ref[span, :] = found
            return carry

        lax.fori_loop(0, channels // 8, step, 0)

    return body


def adjoint_body(levels, channels, rows, width):
    height = rows // levels

    def body(place_ref, d_ref, off_ref, on_ref, top_ref, mate_ref, fold_ref, spread_ref, *refs):
        ups, (out_ref, lines, edges, total) = refs[:levels], refs[levels:]
        lev, odd = place_ref[0], place_ref[1]
        fill(lines, edges, lambda row: d_ref[row].astype(F32), off_ref, on_ref, top_ref, mate_ref, fold_ref, odd, rows, channels, width)
        for hop in range(levels):
            total[pl.ds((lev ^ hop) * height, height)] = ups[hop][...].astype(F32)
        lane = lanes_of((8, width))

        def step(block, carry):
            span = pl.ds(block * 8, 8)
            sums = [None] * rows
            for col in range(TAPS):
                taps = [spread_ref[a * TAPS + col, span, :] for a in range(TAPS)]
                for source in range(rows):
                    moved = shifted(lines[source, span, :], edges[source, span, :], REACH - col, lane, width)
                    for a in range(TAPS):
                        row = source + a - REACH
                        if 0 <= row < rows:
                            term = taps[a] * moved
                            sums[row] = term if sums[row] is None else sums[row] + term
                for source in range(REACH):
                    moved = shifted(lines[rows + source, span, :], edges[rows + source, span, :], col - REACH, lane, width)
                    for depth in range(REACH - source):
                        row = rows - 1 - depth
                        sums[row] = sums[row] + taps[REACH + 1 + depth + source] * moved
            for row in range(rows):
                total[row, span, :] = total[row, span, :] + sums[row]
            return carry

        lax.fori_loop(0, channels // 8, step, 0)
        out_ref[...] = total[...].astype(BF16)

    return body


def across(value, axis, target):
    count = lax.axis_size(axis)
    return lax.ppermute(value, axis, [(i, target(i) % count) for i in range(count)])


def level_swap(blocks):
    return [blocks[0]] + [across(blocks[hop], "lev", lambda i: i ^ hop) for hop in range(1, len(blocks))]


def edge_swap(off, on, top):
    lanes = lax.axis_size("lon")
    near = across(on, "lon", lambda i: i ^ 1)
    far = across(off, "lon", lambda i: i + 1 if i % 2 else i - 1)
    folded = across(top, "lon", lambda i: lanes - 1 - i)
    fold_far = across(off, "lon", lambda i: lanes - 2 - i if i % 2 else lanes - i)
    mate = across(folded, "lon", lambda i: i ^ 1)
    return far, near, folded, mate, fold_far


def shards(snapshot, cotangent, ocean_mask, kernel, norm_gain, norm_shift, weight_in, weight_out):
    levels = lax.axis_size("lev")
    lanes = lax.axis_size("lon")
    channels, rows, width = snapshot.shape
    height = rows // levels
    total_channels = channels * levels
    cells = height * width
    lev = lax.axis_index("lev")
    place = jnp.stack([lev, lax.axis_index("lon") % 2]).astype(jnp.int32)
    groups = groups_of(rows)[0]
    weights = lax.dynamic_slice_in_dim(kernel, lev * channels, channels, 0).astype(F32)
    weights = jnp.pad(weights, ((0, 0), (0, 128 - TAPS * TAPS)))
    block = shaped(height, channels, width)
    pack = shaped(groups, channels, width)
    top_shape = shaped(REACH, channels, width)
    field = pltpu.VMEM((rows, channels, width), F32)
    deep = pltpu.VMEM((rows + REACH, channels, width), F32)
    lines = jnp.swapaxes(snapshot, 0, 1)

    off, on, top, *snap_sends = call(
        prepare_body(levels, channels, rows, width),
        [pack, pack, top_shape] + [block] * (levels - 1),
        [SMEM, VMEM],
        [],
        1.0,
        "prepare",
    )(place, lines)
    snap_edges = edge_swap(off, on, top)
    snaps = level_swap([None] + snap_sends)[1:]
    inner, spread = call(
        inner_body(channels, rows, width),
        [shaped(rows, channels, width, dtype=F32), shaped(TAPS * TAPS, channels, width, dtype=F32)],
        [VMEM] * 2,
        [field],
        3.5,
        "inner",
    )(lines, weights)
    conv_sends = call(
        outer_body(levels, channels, rows, width),
        [block] * levels,
        [SMEM] + [VMEM] * 7,
        [field, pltpu.VMEM((groups, channels, width), F32), pltpu.VMEM((REACH, channels, width), F32)],
        1.5,
        "outer",
    )(place, inner, *snap_edges, spread)
    convs = level_swap(conv_sends)
    upstream, *up_sends = call(
        cotangent_body(levels, channels, height, width),
        [shaped(total_channels, cells)] + [block] * levels,
        [SMEM, VMEM, VMEM],
        [pltpu.VMEM((height, total_channels, width), F32)],
        1.0,
        "cotangent",
    )(place, jnp.swapaxes(cotangent, 0, 1), ocean_mask)
    ups = level_swap(up_sends)
    columns = call(
        columns_body(channels, rows, width),
        shaped(TAPS, rows + REACH, channels, width, dtype=F32),
        [SMEM] + [VMEM] * 6,
        [deep, deep],
        2.0,
        "columns",
    )(place, lines, *snap_edges)
    result, *d_sends = call(
        cell_body(levels, channels, height, width, 512),
        [shaped(height, total_channels, width)] + [block] * levels,
        [SMEM] + [VMEM] * (2 * levels + 6),
        [pltpu.VMEM((total_channels, cells), F32)] * 3,
        5.0,
        "cells",
    )(place, *convs, *snaps, lines, upstream, ocean_mask, norm_gain[:, None], norm_shift[:, None], weight_in, weight_out)
    d_blocks = level_swap(d_sends)
    d_lines, off, on, top = call(
        gather_body(levels, channels, rows, width),
        [shaped(rows, channels, width), pack, pack, top_shape],
        [SMEM] + [VMEM] * levels,
        [field],
        0.8,
        "regroup",
    )(place, *d_blocks)
    d_edges = edge_swap(off, on, top)
    terms = call(
        kernel_body(levels, channels, rows, width),
        shaped(channels, 128, dtype=F32),
        [SMEM] + [VMEM] * (1 + levels),
        [field],
        2.5,
        "kernel_terms",
    )(place, columns, *d_blocks)
    hop = 1
    while hop < lanes:
        terms = terms + across(terms, "lon", lambda i: i ^ hop)
        hop *= 2
    parts = level_swap([terms] * levels)
    stacked = jnp.zeros((levels, channels, 128), F32)
    for hop, part in enumerate(parts):
        stacked = lax.dynamic_update_slice(stacked, part[None], (lev ^ hop, 0, 0))
    kernel_grad = stacked.reshape(total_channels, 128)[:, : TAPS * TAPS]
    d_snapshot = call(
        adjoint_body(levels, channels, rows, width),
        shaped(rows, channels, width),
        [SMEM] + [VMEM] * (7 + levels),
        [deep, deep, field],
        4.0,
        "adjoint",
    )(place, d_lines, *d_edges, spread, *ups)
    return (jnp.swapaxes(result, 0, 1), jnp.swapaxes(d_snapshot, 0, 1), kernel_grad)


def solution(mesh):
    placed = (
        P("lev", None, "lon"),
        P(None, "lev", "lon"),
        P("lev", "lon"),
        P(),
        P(),
        P(),
        P(),
        P(),
    )
    return jax.shard_map(
        shards,
        mesh=mesh,
        in_specs=placed,
        out_specs=(P(None, "lev", "lon"), P("lev", None, "lon"), P()),
        check_vma=False,
    )
```

```python
import jax
import jax.numpy as jnp
from jax import lax
from jax.experimental import pallas as pl
from jax.experimental.pallas import tpu as pltpu
from jax.sharding import PartitionSpec as P

TAPS = 7
REACH = TAPS // 2
EPSILON = 1e-06
ROOT_HALF = 0.7071067811865476
INV_ROOT_TAU = 0.3989422804014327
F32 = jnp.float32
BF16 = jnp.bfloat16
VMEM = pl.BlockSpec(memory_space=pltpu.VMEM)
SMEM = pl.BlockSpec(memory_space=pltpu.SMEM)
SPAN = 2 * REACH
TAP_ROWS = (TAPS * TAPS + 7) // 8 * 8
FIRST = (((0,), (0,)), ((), ()))
LIMIT = 24 * 1024 * 1024


def call(body, out, specs, scratch, micros, name):
    return pl.pallas_call(
        body,
        out_shape=out,
        in_specs=specs,
        out_specs=jax.tree.map(lambda _: VMEM, out),
        scratch_shapes=scratch,
        compiler_params=pltpu.CompilerParams(vmem_limit_bytes=LIMIT),
        cost_estimate=pl.CostEstimate(flops=int(micros * 1.1e9), bytes_accessed=0, transcendentals=0),
        name=name,
    )


def shaped(*shape, dtype=BF16):
    return jax.ShapeDtypeStruct(shape, dtype)


def lanes_of(shape):
    return lax.broadcasted_iota(jnp.int32, shape, len(shape) - 1)


def groups_of(rows):
    per = rows
    while (per + 2 * REACH) * SPAN > 128 or rows % per:
        per -= 1
    return rows // per, per


def ones_where(mask):
    return jnp.where(mask, 1.0, 0.0)


def right_lanes(lane, per, width):
    low = (per + REACH) * SPAN - REACH
    base = SPAN * ((width + SPAN - 1) // SPAN) - width
    place = jnp.where(lane >= low, lane + base, lane)
    return place - SPAN * ((place * 171) >> 10) < REACH


def pack_edges(read, odd, off_ref, on_ref, rows, channels, width):
    count, per = groups_of(rows)
    lane = lanes_of((1, width))
    turn = odd.astype(F32)
    for group in range(count):
        off = jnp.zeros((channels, width), F32)
        on = jnp.zeros((channels, width), F32)
        for place in range(per):
            base = SPAN * place
            line = pltpu.roll(read(group * per + place), base, 1) if place else read(group * per)
            first = ones_where((lane >= base) & (lane < base + REACH))
            spot = (base - REACH) % width
            last = ones_where((lane >= spot) & (lane < spot + REACH))
            off = off + line * (first + turn * (last - first))
            on = on + line * (last + turn * (first - last))
        off_ref[group] = off.astype(BF16)
        on_ref[group] = on.astype(BF16)


def flip_lanes(value, width, top):
    row = lax.broadcasted_iota(jnp.int32, (width, width), 0)
    col = lax.broadcasted_iota(jnp.int32, (width, width), 1)
    exchange = ((row + col == top % width) | (row + col == top % width + width)).astype(BF16)
    return jnp.dot(value, exchange, preferred_element_type=F32)


def flip_fold(lines_of, fold_ref, per, width):
    lane = lanes_of((1, width))
    ends = ones_where((lane >= SPAN * (per - REACH) - REACH) & (lane < SPAN * per - REACH))
    packed = (fold_ref[REACH].astype(F32) * ends).astype(BF16)
    for depth in range(REACH):
        lines_of[depth] = flip_lanes(fold_ref[REACH - 1 - depth], width, width - 1)
    return flip_lanes(packed, width, 2 * SPAN * per - SPAN - 1)


def each_block(channels, step):
    blocks = channels // 8
    unroll = max(n for n in range(1, 5) if blocks % n == 0)
    lax.fori_loop(0, blocks, step, 0, unroll=unroll)


def unpack(group, place, width):
    shift = (-SPAN * place) % width
    return pltpu.roll(group, shift, 1) if shift else group


def fill(lines, edges, read, packs_ref, fold_ref, rows, width):
    per = groups_of(rows)[1]
    folded = flip_fold(lines.at[pl.ds(rows, REACH)], fold_ref, per, width)
    for row in range(rows):
        lines[row] = read(row)
        edges[row] = unpack(packs_ref[row // per], row % per, width)
    for depth in range(REACH):
        edges[rows + depth] = unpack(folded, per + depth, width)


def shifted(line, edge, step, lane, width):
    if step == 0:
        return line
    if step > 0:
        return pltpu.roll(jnp.where(lane < step, edge, line), width - step, 1)
    return pltpu.roll(jnp.where(lane >= width + step, edge, line), -step, 1)


def prepare_body(channels, rows, width):
    def body(place_ref, snap_ref, off_ref, on_ref):
        pack_edges(lambda row: snap_ref[row].astype(F32), place_ref[1], off_ref, on_ref, rows, channels, width)

    return body


def packs_body(channels, rows, width):
    count, per = groups_of(rows)

    def body(place_ref, lines_ref, off_ref, on_ref, packs_ref, fold_ref):
        lane = lanes_of((1, width))
        right = ones_where(right_lanes(lane, per, width))
        near = right + place_ref[1].astype(F32) * (1.0 - 2.0 * right)
        far = 1.0 - near
        for group in range(count):
            value = on_ref[group].astype(F32) * near + off_ref[group].astype(F32) * far
            packs_ref[group] = value
        fold_ref[0:REACH] = lines_ref[rows - REACH :]
        fold_ref[REACH] = value.astype(BF16)

    return body


def inner_body(channels, rows, width):
    def body(snap_ref, weight_ref, out_ref, spread_ref, lines):
        lines[...] = snap_ref[...].astype(F32)
        lane = lanes_of((8, width))

        def step(block, carry):
            span = pl.ds(block * 8, 8)
            weights = weight_ref[span, :]
            sums = [None] * rows
            for col in range(TAPS):
                taps = [jnp.broadcast_to(weights[:, a * TAPS + col : a * TAPS + col + 1], (8, width)) for a in range(TAPS)]
                for a in range(TAPS):
                    spread_ref[a * TAPS + col, span, :] = taps[a]
                for source in range(rows):
                    moved = shifted(lines[source, span, :], 0.0, col - REACH, lane, width)
                    for a in range(TAPS):
                        row = source - a + REACH
                        if 0 <= row < rows:
                            term = taps[a] * moved
                            sums[row] = term if sums[row] is None else sums[row] + term
            for row in range(rows):
                out_ref[row, span, :] = sums[row]
            return carry

        each_block(channels, step)

    return body


def rims_body(channels, rows, width):
    count, per = groups_of(rows)

    def body(inner_ref, packs_ref, spread_ref, out_ref, packed):
        wide = lanes_of((1, width))
        tail = ones_where((wide >= SPAN * (per - REACH) - REACH) & (wide < SPAN * per - REACH))
        begin = ones_where((wide < SPAN * REACH - REACH) | (wide >= width - REACH))
        for group in range(count):
            value = packs_ref[group]
            if group:
                value = value + pltpu.roll(packs_ref[group - 1] * tail, (-SPAN * per) % width, 1)
            if group + 1 < count:
                value = value + pltpu.roll(packs_ref[group + 1] * begin, SPAN * per, 1)
            packed[group] = value
        lane = lanes_of((8, width))
        right = right_lanes(lane, per, width)
        rim = (lane < REACH) | (lane >= width - REACH)

        def step(block, carry):
            span = pl.ds(block * 8, 8)
            for group in range(count):
                near = packed[group, span, :]
                from_right = jnp.where(right, near, 0.0)
                from_left = jnp.where(right, 0.0, near)
                sums = [None, None]
                for a in range(TAPS):
                    for col in range(TAPS):
                        if col == REACH:
                            continue
                        side = col > REACH
                        move = (-(SPAN * (a - REACH) + col - REACH)) % width
                        term = spread_ref[a * TAPS + col, span, :] * pltpu.roll(from_right if side else from_left, move, 1)
                        sums[side] = term if sums[side] is None else sums[side] + term
                rims = jnp.where(right, sums[0], sums[1])
                for place in range(per):
                    row = group * per + place
                    out_ref[row, span, :] = inner_ref[row, span, :] + jnp.where(rim, unpack(rims, place, width), 0.0)
            return carry

        each_block(channels, step)

    return body


def fold_body(levels, channels, rows, width):
    height = rows // levels
    per = groups_of(rows)[1]

    def body(place_ref, part_ref, fold_ref, spread_ref, *rest):
        sends, (total, lines, edges) = rest[:levels], rest[levels:]
        lev = place_ref[0]
        folded = flip_fold(lines, fold_ref, per, width)
        for depth in range(REACH):
            edges[depth] = unpack(folded, per + depth, width)
        lane = lanes_of((8, width))

        def step(block, carry):
            span = pl.ds(block * 8, 8)
            sums = [part_ref[rows - 1 - up, span, :] for up in range(REACH)]
            for depth in range(REACH):
                for col in range(TAPS):
                    moved = shifted(lines[depth, span, :], edges[depth, span, :], col - REACH, lane, width)
                    for up in range(REACH - depth):
                        a = REACH + 1 + depth + up
                        sums[up] = sums[up] + spread_ref[a * TAPS + col, span, :] * moved
            for up in range(REACH):
                total[rows - 1 - up, span, :] = sums[up]
            return carry

        each_block(channels, step)
        total[0 : rows - REACH] = part_ref[0 : rows - REACH]
        for hop in range(levels):
            sends[hop][...] = total[pl.ds((lev ^ hop) * height, height)].astype(BF16)

    return body


def columns_body(channels, rows, width):
    def body(snap_ref, packs_ref, fold_ref, out_ref, lines, edges):
        fill(lines, edges, lambda row: snap_ref[row].astype(F32), packs_ref, fold_ref, rows, width)
        lane = lanes_of((channels, width))
        for col in range(TAPS):
            for source in range(rows + REACH):
                out_ref[col, source] = shifted(lines[source], edges[source], col - REACH, lane, width)

    return body


def cotangent_body(levels, channels, height, width):
    def body(place_ref, snap_ref, cot_ref, mask_ref, up_ref, own_ref, *rest):
        sends, lines = rest[: levels - 1], rest[levels - 1]
        lev = place_ref[0]
        wet = mask_ref[...].astype(F32)
        lines[...] = cot_ref[...].astype(F32) * wet[:, None, :]
        for row in range(height):
            up_ref[:, row * width : (row + 1) * width] = lines[row].astype(BF16)
        for hop in range(levels):
            start = pl.multiple_of((lev ^ hop) * channels, 8)
            for row in range(height):
                value = lines[row, pl.ds(start, channels), :].astype(BF16)
                if hop:
                    sends[hop - 1][height + row] = value
                else:
                    own_ref[row] = value
            if hop:
                sends[hop - 1][0:height] = snap_ref[pl.ds((lev ^ hop) * height, height)]

    return body


def cell_body(levels, channels, height, width, chunk):
    def body(place_ref, *refs):
        convs, refs = refs[:levels], refs[levels:]
        up_ref, gain_ref, shift_ref, win_ref, wout_ref, projected, *refs = refs
        sends, (field, d_lifted) = refs[:levels], refs[levels:]
        lev = place_ref[0]
        for hop in range(levels):
            start = pl.multiple_of((lev ^ hop) * channels, 8)
            for row in range(height):
                field[pl.ds(start, channels), row * width : (row + 1) * width] = convs[hop][row].astype(F32)
        convolved = field[...]
        centre = jnp.mean(convolved, axis=0, keepdims=True)
        centred = convolved - centre
        spread = jnp.mean(centred * centred, axis=0, keepdims=True)
        rstd = lax.rsqrt(spread + EPSILON)
        normed = centred * rstd
        field[...] = normed
        gain = gain_ref[...]
        lifted = (normed * gain + shift_ref[...]).astype(BF16)
        upstream = up_ref[...]
        features = wout_ref.shape[0]
        for piece in range(features // chunk):
            span = slice(piece * chunk, (piece + 1) * chunk)
            hidden = lax.dot_general(win_ref[:, span], lifted, FIRST, preferred_element_type=F32)
            d_active = jnp.dot(wout_ref[span, :], upstream, preferred_element_type=F32)
            half = 0.5 * (1.0 + lax.erf(hidden * ROOT_HALF))
            active = (hidden * half).astype(BF16)
            slope = half + hidden * jnp.exp(-0.5 * hidden * hidden) * INV_ROOT_TAU
            d_hidden = (d_active * slope).astype(BF16)
            out = lax.dot_general(wout_ref[span, :], active, FIRST, preferred_element_type=F32)
            back = jnp.dot(win_ref[:, span], d_hidden, preferred_element_type=F32)
            if piece == 0:
                projected[...] = out
                d_lifted[...] = back
            else:
                projected[...] += out
                d_lifted[...] += back
        d_normed = d_lifted[...] * gain
        normed = field[...]
        first = jnp.mean(d_normed, axis=0, keepdims=True)
        second = jnp.mean(d_normed * normed, axis=0, keepdims=True)
        field[...] = rstd * (d_normed - first - normed * second)
        for hop in range(levels):
            start = pl.multiple_of((lev ^ hop) * channels, 8)
            for row in range(height):
                sends[hop][row] = field[pl.ds(start, channels), row * width : (row + 1) * width].astype(BF16)

    return body


def finish_body(levels, channels, height, width):
    def body(place_ref, snap_ref, mask_ref, projected_ref, *refs):
        others, (result_ref, total) = refs[: levels - 1], refs[levels - 1 :]
        lev = place_ref[0]
        for hop in range(levels):
            start = pl.multiple_of((lev ^ hop) * channels, 8)
            for row in range(height):
                held = others[hop - 1][row] if hop else snap_ref[lev * height + row]
                wet = mask_ref[row : row + 1, :].astype(F32)
                value = held.astype(F32) + projected_ref[pl.ds(start, channels), row * width : (row + 1) * width]
                total[row, pl.ds(start, channels), :] = wet * value
        result_ref[...] = total[...].astype(BF16)

    return body


def gather_body(levels, channels, rows, width):
    height = rows // levels

    def body(place_ref, *refs):
        blocks, (lines_ref, off_ref, on_ref, lines) = refs[:levels], refs[levels:]
        lev, odd = place_ref[0], place_ref[1]
        for hop in range(levels):
            lines[pl.ds((lev ^ hop) * height, height)] = blocks[hop][...].astype(F32)
        lines_ref[...] = lines[...].astype(BF16)
        pack_edges(lambda row: lines[row], odd, off_ref, on_ref, rows, channels, width)

    return body


def kernel_body(levels, channels, rows, width):
    height = rows // levels

    def body(place_ref, columns_ref, *refs):
        blocks, (out_ref, grads, found_ref) = refs[:levels], refs[levels:]
        lev = place_ref[0]
        for hop in range(levels):
            grads[pl.ds((lev ^ hop) * height, height)] = blocks[hop][...].astype(F32)
        out_lane = lanes_of((8, 128))

        def step(block, carry):
            span = pl.ds(block * 8, 8)
            grad = [grads[row, span, :] for row in range(rows)]
            found = jnp.zeros((8, 128), F32)
            for col in range(TAPS):
                sums = [None] * TAPS
                for source in range(rows + REACH):
                    moved = columns_ref[col, source, span, :]
                    for a in range(TAPS):
                        row = source - a + REACH
                        if 0 <= row < rows:
                            term = grad[row] * moved
                            sums[a] = term if sums[a] is None else sums[a] + term
                for a in range(TAPS):
                    found = jnp.where(out_lane == a * TAPS + col, jnp.sum(sums[a], axis=1, keepdims=True), found)
            found_ref[span, :] = found
            return carry

        each_block(channels, step)
        out_ref[:, :channels] = found_ref[...].T[:TAP_ROWS]

    return body


def adjoint_body(levels, channels, rows, width):
    height = rows // levels

    def body(place_ref, d_ref, packs_ref, fold_ref, spread_ref, *refs):
        own_ref, others, (out_ref, lines, edges, total) = refs[0], refs[1:levels], refs[levels:]
        lev = place_ref[0]
        fill(lines, edges, lambda row: d_ref[row].astype(F32), packs_ref, fold_ref, rows, width)
        for hop in range(levels):
            taken = others[hop - 1][height:] if hop else own_ref[...]
            total[pl.ds((lev ^ hop) * height, height)] = taken.astype(F32)
        lane = lanes_of((8, width))

        def step(block, carry):
            span = pl.ds(block * 8, 8)
            sums = [None] * rows
            for col in range(TAPS):
                taps = [spread_ref[a * TAPS + col, span, :] for a in range(TAPS)]
                for source in range(rows):
                    moved = shifted(lines[source, span, :], edges[source, span, :], REACH - col, lane, width)
                    for a in range(TAPS):
                        row = source + a - REACH
                        if 0 <= row < rows:
                            term = taps[a] * moved
                            sums[row] = term if sums[row] is None else sums[row] + term
                for source in range(REACH):
                    moved = shifted(lines[rows + source, span, :], edges[rows + source, span, :], col - REACH, lane, width)
                    for depth in range(REACH - source):
                        row = rows - 1 - depth
                        sums[row] = sums[row] + taps[REACH + 1 + depth + source] * moved
            for row in range(rows):
                total[row, span, :] = total[row, span, :] + sums[row]
            return carry

        each_block(channels, step)
        out_ref[...] = total[...].astype(BF16)

    return body


def across(value, axis, target):
    count = lax.axis_size(axis)
    return lax.ppermute(value, axis, [(i, target(i) % count) for i in range(count)])


def level_swap(blocks):
    return [across(block, "lev", lambda i: i ^ hop) for hop, block in enumerate(blocks, 1)]


def edge_swap(off, on):
    return across(off, "lon", lambda i: i + 1 if i % 2 else i - 1), across(on, "lon", lambda i: i ^ 1)


def mirror(block):
    lanes = lax.axis_size("lon")
    return across(block, "lon", lambda i: lanes - 1 - i)


def by_core(value, moves):
    levels, lanes = lax.axis_size("lev"), lax.axis_size("lon")
    pairs = []
    for lev in range(levels):
        for lon in range(lanes):
            to_lev, to_lon = moves[lon % 2](lev, lon)
            pairs.append((lev * lanes + lon, to_lev * lanes + to_lon))
    return lax.ppermute(value, ("lev", "lon"), pairs)


def fetch_over_lev(terms):
    levels = lax.axis_size("lev")
    got = []
    for hop in range(1, levels, 2):
        other = min(hop + 1, levels - 1)
        got.append(by_core(terms, [lambda v, i: (v ^ hop, i), lambda v, i: (v ^ other, i)]))
    return got, [across(part, "lon", lambda i: i ^ 1) for part in got[:-1]]


def assemble_body(levels, channels):
    count = levels // 2

    def body(place_ref, terms_ref, *refs):
        got, mates, (out_ref, placed) = refs[:count], refs[count : 2 * count - 1], refs[2 * count - 1 :]
        lev, odd = place_ref[0], place_ref[1]
        for hop in range(levels):
            if hop:
                part = (hop - 1) // 2
                value = got[part][...]
                if part < count - 1:
                    mine = odd if hop % 2 == 0 else 1 - odd
                    value = jnp.where(mine == 1, value, mates[part][...])
            else:
                value = terms_ref[...]
            placed[lev ^ hop] = value
        for level in range(levels):
            out_ref[:, level * channels : (level + 1) * channels] = placed[level][: TAPS * TAPS, :channels]

    return body


def shards(snapshot, cotangent, ocean_mask, kernel, norm_gain, norm_shift, weight_in, weight_out):
    levels = lax.axis_size("lev")
    channels, rows, width = snapshot.shape
    height = rows // levels
    total_channels = channels * levels
    cells = height * width
    lev = lax.axis_index("lev")
    odd = lax.axis_index("lon") % 2
    place = jnp.stack([lev, odd]).astype(jnp.int32)
    groups = groups_of(rows)[0]
    weights = lax.dynamic_slice_in_dim(kernel, lev * channels, channels, 0).astype(F32)
    weights = jnp.pad(weights, ((0, 0), (0, 128 - TAPS * TAPS)))
    block = shaped(height, channels, width)
    pack = shaped(groups, channels, width)
    field = pltpu.VMEM((rows, channels, width), F32)
    deep = pltpu.VMEM((rows + REACH, channels, width), F32)
    lines = jnp.swapaxes(snapshot, 0, 1)

    packs_call = call(
        packs_body(channels, rows, width),
        [shaped(groups, channels, width, dtype=F32), shaped(REACH + 1, channels, width)],
        [SMEM] + [VMEM] * 3,
        [],
        0.6,
        "packs",
    )
    off, on = call(prepare_body(channels, rows, width), [pack, pack], [SMEM, VMEM], [], 1.0, "prepare")(place, lines)
    off, on = edge_swap(off, on)
    inner, spread = call(
        inner_body(channels, rows, width),
        [shaped(rows, channels, width, dtype=F32), shaped(TAPS * TAPS, channels, width, dtype=F32)],
        [VMEM] * 2,
        [field],
        3.0,
        "inner",
    )(lines, weights)
    packs, fold = packs_call(place, lines, off, on)
    upstream, up_own, *early_sends = call(
        cotangent_body(levels, channels, height, width),
        [shaped(total_channels, cells), block] + [shaped(2 * height, channels, width)] * (levels - 1),
        [SMEM] + [VMEM] * 3,
        [pltpu.VMEM((height, total_channels, width), F32)],
        1.0,
        "cotangent",
    )(place, lines, jnp.swapaxes(cotangent, 0, 1), ocean_mask)
    early_sends, fold = lax.optimization_barrier((early_sends, fold))
    others = level_swap(early_sends)
    fold = mirror(fold)
    part = call(
        rims_body(channels, rows, width),
        shaped(rows, channels, width, dtype=F32),
        [VMEM] * 3,
        [pltpu.VMEM((groups, channels, width), F32)],
        2.0,
        "rims",
    )(inner, packs, spread)
    conv_own, *conv_sends = call(
        fold_body(levels, channels, rows, width),
        [block] * levels,
        [SMEM] + [VMEM] * 3,
        [field] + [pltpu.VMEM((REACH, channels, width), F32)] * 2,
        1.2,
        "fold",
    )(place, part, fold, spread)
    convs = [conv_own] + level_swap(conv_sends)
    convs, others = lax.optimization_barrier((convs, others))
    columns = call(
        columns_body(channels, rows, width),
        shaped(TAPS, rows + REACH, channels, width, dtype=F32),
        [VMEM] * 3,
        [deep, deep],
        2.0,
        "columns",
    )(lines, packs, fold)
    projected, d_own, *d_sends = call(
        cell_body(levels, channels, height, width, 512),
        [shaped(total_channels, cells, dtype=F32)] + [block] * levels,
        [SMEM] + [VMEM] * (levels + 5),
        [pltpu.VMEM((total_channels, cells), F32)] * 2,
        5.0,
        "cells",
    )(place, *convs, upstream, norm_gain[:, None], norm_shift[:, None], weight_in, weight_out)
    d_blocks = [d_own] + level_swap(d_sends)
    result = call(
        finish_body(levels, channels, height, width),
        shaped(height, total_channels, width),
        [SMEM] + [VMEM] * (levels + 2),
        [pltpu.VMEM((height, total_channels, width), F32)],
        1.0,
        "finish",
    )(place, lines, ocean_mask, projected, *others)
    result, d_blocks = lax.optimization_barrier((result, d_blocks))
    d_lines, off, on = call(
        gather_body(levels, channels, rows, width),
        [shaped(rows, channels, width), pack, pack],
        [SMEM] + [VMEM] * levels,
        [field],
        0.8,
        "regroup",
    )(place, *d_blocks)
    columns, off = lax.optimization_barrier((columns, off))
    terms = call(
        kernel_body(levels, channels, rows, width),
        shaped(TAP_ROWS, 128, dtype=F32),
        [SMEM] + [VMEM] * (1 + levels),
        [field, pltpu.VMEM((channels, 128), F32)],
        0.01,
        "kernel_terms",
    )(place, columns, *d_blocks)
    terms = terms + across(terms, "lon", lambda i: i ^ 1)
    d_packs, d_fold = packs_call(place, d_lines, *edge_swap(off, on))
    terms, d_fold = lax.optimization_barrier((terms, d_fold))
    d_fold = mirror(d_fold)
    terms = terms + across(terms, "lon", lambda i: i ^ 2)
    terms, d_fold = lax.optimization_barrier((terms, d_fold))
    hop = 4
    while hop < lax.axis_size("lon"):
        terms = terms + across(terms, "lon", lambda i: i ^ hop)
        hop *= 2
    d_snapshot = call(
        adjoint_body(levels, channels, rows, width),
        shaped(rows, channels, width),
        [SMEM] + [VMEM] * (4 + levels),
        [deep, deep, field],
        4.0,
        "adjoint",
    )(place, d_lines, d_packs, d_fold, spread, up_own, *others)
    terms, d_snapshot = lax.optimization_barrier((terms, d_snapshot))
    got, mates = fetch_over_lev(terms)
    kernel_grad = call(
        assemble_body(levels, channels),
        shaped(TAPS * TAPS, total_channels, dtype=F32),
        [SMEM] + [VMEM] * (2 * len(got)),
        [pltpu.VMEM((levels, TAP_ROWS, 128), F32)],
        0.8,
        "assemble",
    )(place, terms, *got, *mates)
    return (jnp.swapaxes(result, 0, 1), jnp.swapaxes(d_snapshot, 0, 1), kernel_grad.T)


def solution(mesh):
    placed = (
        P("lev", None, "lon"),
        P(None, "lev", "lon"),
        P("lev", "lon"),
        P(),
        P(),
        P(),
        P(),
        P(),
    )
    return jax.shard_map(
        shards,
        mesh=mesh,
        in_specs=placed,
        out_specs=(P(None, "lev", "lon"), P("lev", None, "lon"), P()),
        check_vma=False,
    )
```

```python
import jax
import jax.numpy as jnp
from jax import lax
from jax.experimental import pallas as pl
from jax.experimental.pallas import tpu as pltpu
from jax.sharding import PartitionSpec as P

TAPS = 7
REACH = TAPS // 2
EPSILON = 1e-06
ROOT_HALF = 0.7071067811865476
INV_ROOT_TAU = 0.3989422804014327
F32 = jnp.float32
BF16 = jnp.bfloat16
VMEM = pl.BlockSpec(memory_space=pltpu.VMEM)
SMEM = pl.BlockSpec(memory_space=pltpu.SMEM)
SPAN = 2 * REACH
TAP_ROWS = (TAPS * TAPS + 7) // 8 * 8
FIRST = (((0,), (0,)), ((), ()))
LIMIT = 24 * 1024 * 1024


def call(body, out, specs, scratch, micros, name):
    return pl.pallas_call(
        body,
        out_shape=out,
        in_specs=specs,
        out_specs=jax.tree.map(lambda _: VMEM, out),
        scratch_shapes=scratch,
        compiler_params=pltpu.CompilerParams(vmem_limit_bytes=LIMIT),
        cost_estimate=pl.CostEstimate(flops=int(micros * 1.1e9), bytes_accessed=0, transcendentals=0),
        name=name,
    )


def shaped(*shape, dtype=BF16):
    return jax.ShapeDtypeStruct(shape, dtype)


def lanes_of(shape):
    return lax.broadcasted_iota(jnp.int32, shape, len(shape) - 1)


def groups_of(rows):
    per = rows
    while (per + 2 * REACH) * SPAN > 128 or rows % per:
        per -= 1
    return rows // per, per


def ones_where(mask):
    return jnp.where(mask, 1.0, 0.0)


def right_lanes(lane, per, width):
    low = (per + REACH) * SPAN - REACH
    base = SPAN * ((width + SPAN - 1) // SPAN) - width
    place = jnp.where(lane >= low, lane + base, lane)
    return place - SPAN * ((place * 171) >> 10) < REACH


def pack_edges(read, odd, off_ref, on_ref, rows, channels, width):
    count, per = groups_of(rows)
    lane = lanes_of((1, width))
    turn = odd.astype(F32)
    for group in range(count):
        off = jnp.zeros((channels, width), F32)
        on = jnp.zeros((channels, width), F32)
        for place in range(per):
            base = SPAN * place
            line = pltpu.roll(read(group * per + place), base, 1) if place else read(group * per)
            first = ones_where((lane >= base) & (lane < base + REACH))
            spot = (base - REACH) % width
            last = ones_where((lane >= spot) & (lane < spot + REACH))
            off = off + line * (first + turn * (last - first))
            on = on + line * (last + turn * (first - last))
        off_ref[group] = off.astype(BF16)
        on_ref[group] = on.astype(BF16)


def flip_lanes(value, width, top):
    row = lax.broadcasted_iota(jnp.int32, (width, width), 0)
    col = lax.broadcasted_iota(jnp.int32, (width, width), 1)
    exchange = ((row + col == top % width) | (row + col == top % width + width)).astype(BF16)
    return jnp.dot(value, exchange, preferred_element_type=F32)


def fold_shape(channels, width):
    parts = 4 if channels % 32 == 0 else 1
    share = channels // parts
    head = (share + 15) // 16 * 16 if parts > 1 else channels
    return ((head + REACH * channels, width) if parts > 1 else (REACH + 1, channels, width)), head, parts


def fold_lanes(per, width):
    lane = lanes_of((1, width))
    begin = SPAN * (per - REACH) - REACH
    return begin, ones_where((lane >= begin) & (lane < SPAN * per - REACH))


def write_fold(fold_ref, value, lines_ref, channels, per, width):
    _, head, parts = fold_shape(channels, width)
    if parts == 1:
        fold_ref[0:REACH] = lines_ref[...]
        fold_ref[REACH] = value.astype(BF16)
        return
    begin, ends = fold_lanes(per, width)
    share = channels // parts
    kept = value * ends
    packed = jnp.zeros((share, width), F32)
    for part in range(parts):
        packed = packed + pltpu.roll(kept[part * share : (part + 1) * share], (part * (width // parts) - begin) % width, 1)
    if head > share:
        packed = jnp.concatenate([packed, jnp.zeros((head - share, width), F32)], axis=0)
    fold_ref[0:head, :] = packed.astype(BF16)
    for row in range(REACH):
        fold_ref[head + row * channels : head + (row + 1) * channels, :] = lines_ref[row]


def flip_fold(lines_of, fold_ref, channels, per, width):
    _, head, parts = fold_shape(channels, width)
    begin, ends = fold_lanes(per, width)
    if parts == 1:
        packed = fold_ref[REACH].astype(F32)
        rows = [fold_ref[row] for row in range(REACH)]
    else:
        held = fold_ref[0:head, :].astype(F32)[: channels // parts]
        pieces = [pltpu.roll(held, (begin - part * (width // parts)) % width, 1) for part in range(parts)]
        packed = jnp.concatenate(pieces, axis=0)
        rows = [fold_ref[head + row * channels : head + (row + 1) * channels, :] for row in range(REACH)]
    for depth in range(REACH):
        lines_of[depth] = flip_lanes(rows[REACH - 1 - depth], width, width - 1)
    return flip_lanes((packed * ends).astype(BF16), width, 2 * SPAN * per - SPAN - 1)


def each_block(channels, step):
    blocks = channels // 8
    unroll = max(n for n in range(1, 5) if blocks % n == 0)
    lax.fori_loop(0, blocks, step, 0, unroll=unroll)


def unpack(group, place, width):
    shift = (-SPAN * place) % width
    return pltpu.roll(group, shift, 1) if shift else group


def fill(lines, edges, read, packs_ref, fold_ref, rows, width):
    per = groups_of(rows)[1]
    folded = flip_fold(lines.at[pl.ds(rows, REACH)], fold_ref, lines.shape[1], per, width)
    for row in range(rows):
        lines[row] = read(row)
        edges[row] = unpack(packs_ref[row // per], row % per, width)
    for depth in range(REACH):
        edges[rows + depth] = unpack(folded, per + depth, width)


def shifted(line, edge, step, lane, width):
    if step == 0:
        return line
    if step > 0:
        return pltpu.roll(jnp.where(lane < step, edge, line), width - step, 1)
    return pltpu.roll(jnp.where(lane >= width + step, edge, line), -step, 1)


def prepare_body(channels, rows, width):
    def body(place_ref, snap_ref, off_ref, on_ref):
        pack_edges(lambda row: snap_ref[row].astype(F32), place_ref[1], off_ref, on_ref, rows, channels, width)

    return body


def packs_body(channels, rows, width):
    count, per = groups_of(rows)

    def body(place_ref, lines_ref, off_ref, on_ref, packs_ref, fold_ref):
        lane = lanes_of((1, width))
        right = ones_where(right_lanes(lane, per, width))
        near = right + place_ref[1].astype(F32) * (1.0 - 2.0 * right)
        far = 1.0 - near
        for group in range(count):
            value = on_ref[group].astype(F32) * near + off_ref[group].astype(F32) * far
            packs_ref[group] = value
        write_fold(fold_ref, value, lines_ref.at[pl.ds(rows - REACH, REACH)], channels, per, width)

    return body


def inner_body(channels, rows, width):
    def body(snap_ref, weight_ref, out_ref, spread_ref, lines):
        lines[...] = snap_ref[...].astype(F32)
        lane = lanes_of((8, width))

        def step(block, carry):
            span = pl.ds(block * 8, 8)
            weights = weight_ref[span, :]
            sums = [None] * rows
            for col in range(TAPS):
                taps = [jnp.broadcast_to(weights[:, a * TAPS + col : a * TAPS + col + 1], (8, width)) for a in range(TAPS)]
                for a in range(TAPS):
                    spread_ref[a * TAPS + col, span, :] = taps[a]
                for source in range(rows):
                    moved = shifted(lines[source, span, :], 0.0, col - REACH, lane, width)
                    for a in range(TAPS):
                        row = source - a + REACH
                        if 0 <= row < rows:
                            term = taps[a] * moved
                            sums[row] = term if sums[row] is None else sums[row] + term
            for row in range(rows):
                out_ref[row, span, :] = sums[row]
            return carry

        each_block(channels, step)

    return body


def rims_body(channels, rows, width):
    count, per = groups_of(rows)

    def body(inner_ref, packs_ref, spread_ref, out_ref, packed):
        wide = lanes_of((1, width))
        tail = ones_where((wide >= SPAN * (per - REACH) - REACH) & (wide < SPAN * per - REACH))
        begin = ones_where((wide < SPAN * REACH - REACH) | (wide >= width - REACH))
        for group in range(count):
            value = packs_ref[group]
            if group:
                value = value + pltpu.roll(packs_ref[group - 1] * tail, (-SPAN * per) % width, 1)
            if group + 1 < count:
                value = value + pltpu.roll(packs_ref[group + 1] * begin, SPAN * per, 1)
            packed[group] = value
        lane = lanes_of((8, width))
        right = right_lanes(lane, per, width)
        rim = (lane < REACH) | (lane >= width - REACH)

        def step(block, carry):
            span = pl.ds(block * 8, 8)
            for group in range(count):
                near = packed[group, span, :]
                from_right = jnp.where(right, near, 0.0)
                from_left = jnp.where(right, 0.0, near)
                sums = [None, None]
                for a in range(TAPS):
                    for col in range(TAPS):
                        if col == REACH:
                            continue
                        side = col > REACH
                        move = (-(SPAN * (a - REACH) + col - REACH)) % width
                        term = spread_ref[a * TAPS + col, span, :] * pltpu.roll(from_right if side else from_left, move, 1)
                        sums[side] = term if sums[side] is None else sums[side] + term
                rims = jnp.where(right, sums[0], sums[1])
                for place in range(per):
                    row = group * per + place
                    out_ref[row, span, :] = inner_ref[row, span, :] + jnp.where(rim, unpack(rims, place, width), 0.0)
            return carry

        each_block(channels, step)

    return body


def fold_body(levels, channels, rows, width):
    height = rows // levels
    per = groups_of(rows)[1]

    def body(place_ref, part_ref, fold_ref, spread_ref, *rest):
        sends, (total, lines, edges) = rest[:levels], rest[levels:]
        lev = place_ref[0]
        folded = flip_fold(lines, fold_ref, channels, per, width)
        for depth in range(REACH):
            edges[depth] = unpack(folded, per + depth, width)
        lane = lanes_of((8, width))

        def step(block, carry):
            span = pl.ds(block * 8, 8)
            sums = [part_ref[rows - 1 - up, span, :] for up in range(REACH)]
            for depth in range(REACH):
                for col in range(TAPS):
                    moved = shifted(lines[depth, span, :], edges[depth, span, :], col - REACH, lane, width)
                    for up in range(REACH - depth):
                        a = REACH + 1 + depth + up
                        sums[up] = sums[up] + spread_ref[a * TAPS + col, span, :] * moved
            for up in range(REACH):
                total[rows - 1 - up, span, :] = sums[up]
            return carry

        each_block(channels, step)
        total[0 : rows - REACH] = part_ref[0 : rows - REACH]
        for hop in range(levels):
            sends[hop][...] = total[pl.ds((lev ^ hop) * height, height)].astype(BF16)

    return body


def columns_body(channels, rows, width):
    def body(snap_ref, packs_ref, fold_ref, out_ref, lines, edges):
        fill(lines, edges, lambda row: snap_ref[row].astype(F32), packs_ref, fold_ref, rows, width)
        lane = lanes_of((channels, width))
        for col in range(TAPS):
            for source in range(rows + REACH):
                out_ref[col, source] = shifted(lines[source], edges[source], col - REACH, lane, width)

    return body


def cotangent_body(levels, channels, height, width):
    def body(place_ref, snap_ref, cot_ref, mask_ref, up_ref, own_ref, *rest):
        sends, lines = rest[: levels - 1], rest[levels - 1]
        lev = place_ref[0]
        wet = mask_ref[...].astype(F32)
        lines[...] = cot_ref[...].astype(F32) * wet[:, None, :]
        for row in range(height):
            up_ref[:, row * width : (row + 1) * width] = lines[row].astype(BF16)
        for hop in range(levels):
            start = pl.multiple_of((lev ^ hop) * channels, 8)
            for row in range(height):
                value = lines[row, pl.ds(start, channels), :].astype(BF16)
                if hop:
                    sends[hop - 1][height + row] = value
                else:
                    own_ref[row] = value
            if hop:
                sends[hop - 1][0:height] = snap_ref[pl.ds((lev ^ hop) * height, height)]

    return body


def cell_body(levels, channels, height, width, chunk):
    def body(place_ref, *refs):
        convs, refs = refs[:levels], refs[levels:]
        up_ref, gain_ref, shift_ref, win_ref, wout_ref, projected, *refs = refs
        sends, (field, d_lifted) = refs[:levels], refs[levels:]
        lev = place_ref[0]
        for hop in range(levels):
            start = pl.multiple_of((lev ^ hop) * channels, 8)
            for row in range(height):
                field[pl.ds(start, channels), row * width : (row + 1) * width] = convs[hop][row].astype(F32)
        convolved = field[...]
        centre = jnp.mean(convolved, axis=0, keepdims=True)
        centred = convolved - centre
        spread = jnp.mean(centred * centred, axis=0, keepdims=True)
        rstd = lax.rsqrt(spread + EPSILON)
        normed = centred * rstd
        field[...] = normed
        gain = gain_ref[...]
        lifted = (normed * gain + shift_ref[...]).astype(BF16)
        upstream = up_ref[...]
        features = wout_ref.shape[0]
        for piece in range(features // chunk):
            span = slice(piece * chunk, (piece + 1) * chunk)
            hidden = lax.dot_general(win_ref[:, span], lifted, FIRST, preferred_element_type=F32)
            d_active = jnp.dot(wout_ref[span, :], upstream, preferred_element_type=F32)
            half = 0.5 * (1.0 + lax.erf(hidden * ROOT_HALF))
            active = (hidden * half).astype(BF16)
            slope = half + hidden * jnp.exp(-0.5 * hidden * hidden) * INV_ROOT_TAU
            d_hidden = (d_active * slope).astype(BF16)
            out = lax.dot_general(wout_ref[span, :], active, FIRST, preferred_element_type=F32)
            back = jnp.dot(win_ref[:, span], d_hidden, preferred_element_type=F32)
            if piece == 0:
                projected[...] = out
                d_lifted[...] = back
            else:
                projected[...] += out
                d_lifted[...] += back
        d_normed = d_lifted[...] * gain
        normed = field[...]
        first = jnp.mean(d_normed, axis=0, keepdims=True)
        second = jnp.mean(d_normed * normed, axis=0, keepdims=True)
        field[...] = rstd * (d_normed - first - normed * second)
        for hop in range(levels):
            start = pl.multiple_of((lev ^ hop) * channels, 8)
            for row in range(height):
                sends[hop][row] = field[pl.ds(start, channels), row * width : (row + 1) * width].astype(BF16)

    return body


def finish_body(levels, channels, height, width):
    def body(place_ref, snap_ref, mask_ref, projected_ref, *refs):
        others, (result_ref, total) = refs[: levels - 1], refs[levels - 1 :]
        lev = place_ref[0]
        for hop in range(levels):
            start = pl.multiple_of((lev ^ hop) * channels, 8)
            for row in range(height):
                held = others[hop - 1][row] if hop else snap_ref[lev * height + row]
                wet = mask_ref[row : row + 1, :].astype(F32)
                value = held.astype(F32) + projected_ref[pl.ds(start, channels), row * width : (row + 1) * width]
                total[row, pl.ds(start, channels), :] = wet * value
        result_ref[...] = total[...].astype(BF16)

    return body


def gather_body(levels, channels, rows, width):
    height = rows // levels

    def body(place_ref, *refs):
        blocks, (lines_ref, off_ref, on_ref, lines) = refs[:levels], refs[levels:]
        lev, odd = place_ref[0], place_ref[1]
        for hop in range(levels):
            lines[pl.ds((lev ^ hop) * height, height)] = blocks[hop][...].astype(F32)
        lines_ref[...] = lines[...].astype(BF16)
        pack_edges(lambda row: lines[row], odd, off_ref, on_ref, rows, channels, width)

    return body


def kernel_body(levels, channels, rows, width):
    height = rows // levels

    def body(place_ref, columns_ref, *refs):
        blocks, (out_ref, grads, found_ref) = refs[:levels], refs[levels:]
        lev = place_ref[0]
        for hop in range(levels):
            grads[pl.ds((lev ^ hop) * height, height)] = blocks[hop][...].astype(F32)
        out_lane = lanes_of((8, 128))

        def step(block, carry):
            span = pl.ds(block * 8, 8)
            grad = [grads[row, span, :] for row in range(rows)]
            found = jnp.zeros((8, 128), F32)
            for col in range(TAPS):
                sums = [None] * TAPS
                for source in range(rows + REACH):
                    moved = columns_ref[col, source, span, :]
                    for a in range(TAPS):
                        row = source - a + REACH
                        if 0 <= row < rows:
                            term = grad[row] * moved
                            sums[a] = term if sums[a] is None else sums[a] + term
                for a in range(TAPS):
                    found = jnp.where(out_lane == a * TAPS + col, jnp.sum(sums[a], axis=1, keepdims=True), found)
            found_ref[span, :] = found
            return carry

        each_block(channels, step)
        out_ref[:, :channels] = found_ref[...].T[:TAP_ROWS]

    return body


def adjoint_body(levels, channels, rows, width):
    height = rows // levels

    def body(place_ref, d_ref, packs_ref, fold_ref, spread_ref, *refs):
        own_ref, others, (out_ref, lines, edges, total) = refs[0], refs[1:levels], refs[levels:]
        lev = place_ref[0]
        fill(lines, edges, lambda row: d_ref[row].astype(F32), packs_ref, fold_ref, rows, width)
        for hop in range(levels):
            taken = others[hop - 1][height:] if hop else own_ref[...]
            total[pl.ds((lev ^ hop) * height, height)] = taken.astype(F32)
        lane = lanes_of((8, width))

        def step(block, carry):
            span = pl.ds(block * 8, 8)
            sums = [None] * rows
            for col in range(TAPS):
                taps = [spread_ref[a * TAPS + col, span, :] for a in range(TAPS)]
                for source in range(rows):
                    moved = shifted(lines[source, span, :], edges[source, span, :], REACH - col, lane, width)
                    for a in range(TAPS):
                        row = source + a - REACH
                        if 0 <= row < rows:
                            term = taps[a] * moved
                            sums[row] = term if sums[row] is None else sums[row] + term
                for source in range(REACH):
                    moved = shifted(lines[rows + source, span, :], edges[rows + source, span, :], col - REACH, lane, width)
                    for depth in range(REACH - source):
                        row = rows - 1 - depth
                        sums[row] = sums[row] + taps[REACH + 1 + depth + source] * moved
            for row in range(rows):
                total[row, span, :] = total[row, span, :] + sums[row]
            return carry

        each_block(channels, step)
        out_ref[...] = total[...].astype(BF16)

    return body


def across(value, axis, target):
    count = lax.axis_size(axis)
    return lax.ppermute(value, axis, [(i, target(i) % count) for i in range(count)])


def level_swap(blocks):
    return [across(block, "lev", lambda i: i ^ hop) for hop, block in enumerate(blocks, 1)]


def edge_swap(off, on):
    return across(off, "lon", lambda i: i + 1 if i % 2 else i - 1), across(on, "lon", lambda i: i ^ 1)


def mirror(block):
    lanes = lax.axis_size("lon")
    return across(block, "lon", lambda i: lanes - 1 - i)


def sum_over_chips(terms):
    lanes = lax.axis_size("lon")
    hop = 2
    while hop < lanes:
        if 2 * hop < lanes:
            one, two, three = (across(terms, "lon", lambda i: i ^ (n * hop)) for n in (1, 2, 3))
            terms = (terms + one) + (two + three)
        else:
            terms = terms + across(terms, "lon", lambda i: i ^ hop)
        hop *= 4
    return terms


def assemble_body(levels, channels):
    def body(place_ref, *refs):
        parts, (out_ref, placed) = refs[:levels], refs[levels:]
        lev = place_ref[0]
        for hop in range(levels):
            placed[lev ^ hop] = parts[hop][...]
        for level in range(levels):
            out_ref[:, level * channels : (level + 1) * channels] = placed[level][: TAPS * TAPS, :channels]

    return body


def shards(snapshot, cotangent, ocean_mask, kernel, norm_gain, norm_shift, weight_in, weight_out):
    levels = lax.axis_size("lev")
    channels, rows, width = snapshot.shape
    height = rows // levels
    total_channels = channels * levels
    cells = height * width
    lev = lax.axis_index("lev")
    odd = lax.axis_index("lon") % 2
    place = jnp.stack([lev, odd]).astype(jnp.int32)
    groups = groups_of(rows)[0]
    weights = lax.dynamic_slice_in_dim(kernel, lev * channels, channels, 0).astype(F32)
    weights = jnp.pad(weights, ((0, 0), (0, 128 - TAPS * TAPS)))
    block = shaped(height, channels, width)
    pack = shaped(groups, channels, width)
    field = pltpu.VMEM((rows, channels, width), F32)
    deep = pltpu.VMEM((rows + REACH, channels, width), F32)
    lines = jnp.swapaxes(snapshot, 0, 1)

    packs_call = call(
        packs_body(channels, rows, width),
        [shaped(groups, channels, width, dtype=F32), shaped(*fold_shape(channels, width)[0])],
        [SMEM] + [VMEM] * 3,
        [],
        0.6,
        "packs",
    )
    off, on = call(prepare_body(channels, rows, width), [pack, pack], [SMEM, VMEM], [], 1.0, "prepare")(place, lines)
    off, on = edge_swap(off, on)
    inner, spread = call(
        inner_body(channels, rows, width),
        [shaped(rows, channels, width, dtype=F32), shaped(TAPS * TAPS, channels, width, dtype=F32)],
        [VMEM] * 2,
        [field],
        3.0,
        "inner",
    )(lines, weights)
    packs, fold = packs_call(place, lines, off, on)
    upstream, up_own, *early_sends = call(
        cotangent_body(levels, channels, height, width),
        [shaped(total_channels, cells), block] + [shaped(2 * height, channels, width)] * (levels - 1),
        [SMEM] + [VMEM] * 3,
        [pltpu.VMEM((height, total_channels, width), F32)],
        1.0,
        "cotangent",
    )(place, lines, jnp.swapaxes(cotangent, 0, 1), ocean_mask)
    early_sends, fold = lax.optimization_barrier((early_sends, fold))
    others = level_swap(early_sends)
    fold = mirror(fold)
    part = call(
        rims_body(channels, rows, width),
        shaped(rows, channels, width, dtype=F32),
        [VMEM] * 3,
        [pltpu.VMEM((groups, channels, width), F32)],
        2.0,
        "rims",
    )(inner, packs, spread)
    conv_own, *conv_sends = call(
        fold_body(levels, channels, rows, width),
        [block] * levels,
        [SMEM] + [VMEM] * 3,
        [field] + [pltpu.VMEM((REACH, channels, width), F32)] * 2,
        1.2,
        "fold",
    )(place, part, fold, spread)
    convs = [conv_own] + level_swap(conv_sends)
    convs, others = lax.optimization_barrier((convs, others))
    columns = call(
        columns_body(channels, rows, width),
        shaped(TAPS, rows + REACH, channels, width, dtype=F32),
        [VMEM] * 3,
        [deep, deep],
        2.0,
        "columns",
    )(lines, packs, fold)
    projected, d_own, *d_sends = call(
        cell_body(levels, channels, height, width, 512),
        [shaped(total_channels, cells, dtype=F32)] + [block] * levels,
        [SMEM] + [VMEM] * (levels + 5),
        [pltpu.VMEM((total_channels, cells), F32)] * 2,
        5.0,
        "cells",
    )(place, *convs, upstream, norm_gain[:, None], norm_shift[:, None], weight_in, weight_out)
    d_blocks = [d_own] + level_swap(d_sends)
    result = call(
        finish_body(levels, channels, height, width),
        shaped(height, total_channels, width),
        [SMEM] + [VMEM] * (levels + 2),
        [pltpu.VMEM((height, total_channels, width), F32)],
        1.0,
        "finish",
    )(place, lines, ocean_mask, projected, *others)
    result, d_blocks = lax.optimization_barrier((result, d_blocks))
    d_lines, off, on = call(
        gather_body(levels, channels, rows, width),
        [shaped(rows, channels, width), pack, pack],
        [SMEM] + [VMEM] * levels,
        [field],
        0.8,
        "regroup",
    )(place, *d_blocks)
    columns, off = lax.optimization_barrier((columns, off))
    terms = call(
        kernel_body(levels, channels, rows, width),
        shaped(TAP_ROWS, 128, dtype=F32),
        [SMEM] + [VMEM] * (1 + levels),
        [field, pltpu.VMEM((channels, 128), F32)],
        0.01,
        "kernel_terms",
    )(place, columns, *d_blocks)
    terms = terms + across(terms, "lon", lambda i: i ^ 1)
    d_packs, d_fold = packs_call(place, d_lines, *edge_swap(off, on))
    terms, d_fold = lax.optimization_barrier((terms, d_fold))
    d_fold = mirror(d_fold)
    terms = sum_over_chips(terms)
    d_snapshot = call(
        adjoint_body(levels, channels, rows, width),
        shaped(rows, channels, width),
        [SMEM] + [VMEM] * (4 + levels),
        [deep, deep, field],
        4.0,
        "adjoint",
    )(place, d_lines, d_packs, d_fold, spread, up_own, *others)
    others = level_swap([terms] * (levels - 1))
    others, _ = lax.optimization_barrier((others, d_snapshot))
    kernel_grad = call(
        assemble_body(levels, channels),
        shaped(TAPS * TAPS, total_channels, dtype=F32),
        [SMEM] + [VMEM] * levels,
        [pltpu.VMEM((levels, TAP_ROWS, 128), F32)],
        0.8,
        "assemble",
    )(place, terms, *others)
    return (jnp.swapaxes(result, 0, 1), jnp.swapaxes(d_snapshot, 0, 1), kernel_grad.T)


def solution(mesh):
    placed = (
        P("lev", None, "lon"),
        P(None, "lev", "lon"),
        P("lev", "lon"),
        P(),
        P(),
        P(),
        P(),
        P(),
    )
    return jax.shard_map(
        shards,
        mesh=mesh,
        in_specs=placed,
        out_specs=(P(None, "lev", "lon"), P("lev", None, "lon"), P()),
        check_vma=False,
    )
```

```python
import jax
import jax.numpy as jnp
from jax import lax
from jax.experimental import pallas as pl
from jax.experimental.pallas import tpu as pltpu
from jax.sharding import PartitionSpec as P

TAPS = 7
REACH = TAPS // 2
EPSILON = 1e-06
ROOT_HALF = 0.7071067811865476
INV_ROOT_TAU = 0.3989422804014327
F32 = jnp.float32
BF16 = jnp.bfloat16
VMEM = pl.BlockSpec(memory_space=pltpu.VMEM)
SMEM = pl.BlockSpec(memory_space=pltpu.SMEM)
SPAN = 2 * REACH
TAP_ROWS = (TAPS * TAPS + 7) // 8 * 8
FIRST = (((0,), (0,)), ((), ()))
LIMIT = 24 * 1024 * 1024


def call(body, out, specs, scratch, micros, name):
    return pl.pallas_call(
        body,
        out_shape=out,
        in_specs=specs,
        out_specs=jax.tree.map(lambda _: VMEM, out),
        scratch_shapes=scratch,
        compiler_params=pltpu.CompilerParams(vmem_limit_bytes=LIMIT),
        cost_estimate=pl.CostEstimate(flops=int(micros * 1.1e9), bytes_accessed=0, transcendentals=0),
        name=name,
    )


def shaped(*shape, dtype=BF16):
    return jax.ShapeDtypeStruct(shape, dtype)


def lanes_of(shape):
    return lax.broadcasted_iota(jnp.int32, shape, len(shape) - 1)


def groups_of(rows):
    per = rows
    while (per + 2 * REACH) * SPAN > 128 or rows % per:
        per -= 1
    return rows // per, per


def ones_where(mask):
    return jnp.where(mask, 1.0, 0.0)


def right_lanes(lane, per, width):
    low = (per + REACH) * SPAN - REACH
    base = SPAN * ((width + SPAN - 1) // SPAN) - width
    place = jnp.where(lane >= low, lane + base, lane)
    return place - SPAN * ((place * 171) >> 10) < REACH


def pack_edges(read, odd, off_ref, on_ref, rows, channels, width):
    count, per = groups_of(rows)
    lane = lanes_of((1, width))
    turn = odd.astype(F32)
    for group in range(count):
        off = jnp.zeros((channels, width), F32)
        on = jnp.zeros((channels, width), F32)
        for place in range(per):
            base = SPAN * place
            line = pltpu.roll(read(group * per + place), base, 1) if place else read(group * per)
            first = ones_where((lane >= base) & (lane < base + REACH))
            spot = (base - REACH) % width
            last = ones_where((lane >= spot) & (lane < spot + REACH))
            off = off + line * (first + turn * (last - first))
            on = on + line * (last + turn * (first - last))
        off_ref[group] = off.astype(BF16)
        on_ref[group] = on.astype(BF16)


def flip_lanes(value, width, top):
    row = lax.broadcasted_iota(jnp.int32, (width, width), 0)
    col = lax.broadcasted_iota(jnp.int32, (width, width), 1)
    exchange = ((row + col == top % width) | (row + col == top % width + width)).astype(BF16)
    return jnp.dot(value, exchange, preferred_element_type=F32)


def fold_shape(channels, width):
    parts = 4 if channels % 32 == 0 else 1
    share = channels // parts
    head = (share + 15) // 16 * 16 if parts > 1 else channels
    return ((head + REACH * channels, width) if parts > 1 else (REACH + 1, channels, width)), head, parts


def fold_lanes(per, width):
    lane = lanes_of((1, width))
    begin = SPAN * (per - REACH) - REACH
    return begin, ones_where((lane >= begin) & (lane < SPAN * per - REACH))


def write_fold(fold_ref, value, lines_ref, channels, per, width):
    _, head, parts = fold_shape(channels, width)
    if parts == 1:
        fold_ref[0:REACH] = lines_ref[...]
        fold_ref[REACH] = value.astype(BF16)
        return
    begin, ends = fold_lanes(per, width)
    share = channels // parts
    kept = value * ends
    packed = jnp.zeros((share, width), F32)
    for part in range(parts):
        packed = packed + pltpu.roll(kept[part * share : (part + 1) * share], (part * (width // parts) - begin) % width, 1)
    if head > share:
        packed = jnp.concatenate([packed, jnp.zeros((head - share, width), F32)], axis=0)
    fold_ref[0:head, :] = packed.astype(BF16)
    for row in range(REACH):
        fold_ref[head + row * channels : head + (row + 1) * channels, :] = lines_ref[row]


def flip_fold(lines_of, fold_ref, channels, per, width):
    _, head, parts = fold_shape(channels, width)
    begin, ends = fold_lanes(per, width)
    if parts == 1:
        packed = fold_ref[REACH].astype(F32)
        for depth in range(REACH):
            lines_of[depth] = flip_lanes(fold_ref[REACH - 1 - depth], width, width - 1)
    else:
        held = fold_ref[0:head, :].astype(F32)[: channels // parts]
        pieces = [pltpu.roll(held, (begin - part * (width // parts)) % width, 1) for part in range(parts)]
        packed = jnp.concatenate(pieces, axis=0)
        flipped = flip_lanes(fold_ref[head : head + REACH * channels, :], width, width - 1)
        for depth in range(REACH):
            row = REACH - 1 - depth
            lines_of[depth] = flipped[row * channels : (row + 1) * channels]
    return flip_lanes((packed * ends).astype(BF16), width, 2 * SPAN * per - SPAN - 1)


def each_block(channels, step):
    blocks = channels // 8
    unroll = max(n for n in range(1, 5) if blocks % n == 0)
    lax.fori_loop(0, blocks, step, 0, unroll=unroll)


def unpack(group, place, width):
    shift = (-SPAN * place) % width
    return pltpu.roll(group, shift, 1) if shift else group


def fill(lines, edges, read, packs_ref, fold_ref, rows, width):
    per = groups_of(rows)[1]
    folded = flip_fold(lines.at[pl.ds(rows, REACH)], fold_ref, lines.shape[1], per, width)
    for row in range(rows):
        lines[row] = read(row)
        edges[row] = unpack(packs_ref[row // per], row % per, width)
    for depth in range(REACH):
        edges[rows + depth] = unpack(folded, per + depth, width)


def shifted(line, edge, step, lane, width):
    if step == 0:
        return line
    if step > 0:
        return pltpu.roll(jnp.where(lane < step, edge, line), width - step, 1)
    return pltpu.roll(jnp.where(lane >= width + step, edge, line), -step, 1)


def prepare_body(channels, rows, width):
    def body(place_ref, snap_ref, off_ref, on_ref):
        pack_edges(lambda row: snap_ref[row].astype(F32), place_ref[1], off_ref, on_ref, rows, channels, width)

    return body


def packs_body(channels, rows, width):
    count, per = groups_of(rows)

    def body(place_ref, lines_ref, off_ref, on_ref, packs_ref, fold_ref):
        lane = lanes_of((1, width))
        right = ones_where(right_lanes(lane, per, width))
        near = right + place_ref[1].astype(F32) * (1.0 - 2.0 * right)
        far = 1.0 - near
        for group in range(count):
            value = on_ref[group].astype(F32) * near + off_ref[group].astype(F32) * far
            packs_ref[group] = value
        write_fold(fold_ref, value, lines_ref.at[pl.ds(rows - REACH, REACH)], channels, per, width)

    return body


def inner_body(channels, rows, width):
    def body(snap_ref, weight_ref, out_ref, spread_ref, lines):
        lines[...] = snap_ref[...].astype(F32)
        weights = weight_ref[...].astype(BF16)
        row = lax.broadcasted_iota(jnp.int32, (128, 2 * width), 0)
        second = jnp.where(lax.broadcasted_iota(jnp.int32, (128, 2 * width), 1) < width, 0, 1)
        for tap in range(0, TAPS * TAPS, 2):
            pick = jnp.where(row == second + tap, 1.0, 0.0).astype(BF16)
            pair = jnp.dot(weights, pick, preferred_element_type=F32)
            spread_ref[tap] = pair[:, :width]
            if tap + 1 < TAPS * TAPS:
                spread_ref[tap + 1] = pair[:, width:]
        lane = lanes_of((8, width))

        def step(block, carry):
            span = pl.ds(block * 8, 8)
            sums = [None] * rows
            for col in range(TAPS):
                taps = [spread_ref[a * TAPS + col, span, :] for a in range(TAPS)]
                for source in range(rows):
                    moved = shifted(lines[source, span, :], 0.0, col - REACH, lane, width)
                    for a in range(TAPS):
                        row = source - a + REACH
                        if 0 <= row < rows:
                            term = taps[a] * moved
                            sums[row] = term if sums[row] is None else sums[row] + term
            for row in range(rows):
                out_ref[row, span, :] = sums[row]
            return carry

        each_block(channels, step)

    return body


def rims_body(channels, rows, width):
    count, per = groups_of(rows)

    def body(inner_ref, packs_ref, spread_ref, out_ref, packed):
        wide = lanes_of((1, width))
        tail = ones_where((wide >= SPAN * (per - REACH) - REACH) & (wide < SPAN * per - REACH))
        begin = ones_where((wide < SPAN * REACH - REACH) | (wide >= width - REACH))
        for group in range(count):
            value = packs_ref[group]
            if group:
                value = value + pltpu.roll(packs_ref[group - 1] * tail, (-SPAN * per) % width, 1)
            if group + 1 < count:
                value = value + pltpu.roll(packs_ref[group + 1] * begin, SPAN * per, 1)
            packed[group] = value
        lane = lanes_of((8, width))
        right = right_lanes(lane, per, width)
        rim = (lane < REACH) | (lane >= width - REACH)

        def step(block, carry):
            span = pl.ds(block * 8, 8)
            for group in range(count):
                near = packed[group, span, :]
                from_right = jnp.where(right, near, 0.0)
                from_left = jnp.where(right, 0.0, near)
                sums = [None, None]
                for a in range(TAPS):
                    for col in range(TAPS):
                        if col == REACH:
                            continue
                        side = col > REACH
                        move = (-(SPAN * (a - REACH) + col - REACH)) % width
                        term = spread_ref[a * TAPS + col, span, :] * pltpu.roll(from_right if side else from_left, move, 1)
                        sums[side] = term if sums[side] is None else sums[side] + term
                rims = jnp.where(right, sums[0], sums[1])
                for place in range(per):
                    row = group * per + place
                    out_ref[row, span, :] = inner_ref[row, span, :] + jnp.where(rim, unpack(rims, place, width), 0.0)
            return carry

        each_block(channels, step)

    return body


def fold_body(levels, channels, rows, width):
    height = rows // levels
    per = groups_of(rows)[1]

    def body(place_ref, part_ref, fold_ref, spread_ref, *rest):
        sends, (total, lines, edges) = rest[:levels], rest[levels:]
        lev = place_ref[0]
        folded = flip_fold(lines, fold_ref, channels, per, width)
        for depth in range(REACH):
            edges[depth] = unpack(folded, per + depth, width)
        lane = lanes_of((8, width))

        def step(block, carry):
            span = pl.ds(block * 8, 8)
            sums = [part_ref[rows - 1 - up, span, :] for up in range(REACH)]
            for depth in range(REACH):
                for col in range(TAPS):
                    moved = shifted(lines[depth, span, :], edges[depth, span, :], col - REACH, lane, width)
                    for up in range(REACH - depth):
                        a = REACH + 1 + depth + up
                        sums[up] = sums[up] + spread_ref[a * TAPS + col, span, :] * moved
            for up in range(REACH):
                total[rows - 1 - up, span, :] = sums[up]
            return carry

        each_block(channels, step)
        total[0 : rows - REACH] = part_ref[0 : rows - REACH]
        for hop in range(levels):
            sends[hop][...] = total[pl.ds((lev ^ hop) * height, height)].astype(BF16)

    return body


def columns_body(channels, rows, width):
    def body(snap_ref, packs_ref, fold_ref, out_ref, lines, edges):
        fill(lines, edges, lambda row: snap_ref[row].astype(F32), packs_ref, fold_ref, rows, width)
        lane = lanes_of((channels, width))
        for col in range(TAPS):
            for source in range(rows + REACH):
                out_ref[col, source] = shifted(lines[source], edges[source], col - REACH, lane, width)

    return body


def cotangent_body(levels, channels, height, width):
    def body(place_ref, snap_ref, cot_ref, mask_ref, up_ref, own_ref, *rest):
        sends, lines = rest[: levels - 1], rest[levels - 1]
        lev = place_ref[0]
        wet = mask_ref[...].astype(F32)
        lines[...] = cot_ref[...].astype(F32) * wet[:, None, :]
        for row in range(height):
            up_ref[:, row * width : (row + 1) * width] = lines[row].astype(BF16)
        for hop in range(levels):
            start = pl.multiple_of((lev ^ hop) * channels, 8)
            for row in range(height):
                value = lines[row, pl.ds(start, channels), :].astype(BF16)
                if hop:
                    sends[hop - 1][height + row] = value
                else:
                    own_ref[row] = value
            if hop:
                sends[hop - 1][0:height] = snap_ref[pl.ds((lev ^ hop) * height, height)]

    return body


def cell_body(levels, channels, height, width, chunk):
    def body(place_ref, *refs):
        convs, refs = refs[:levels], refs[levels:]
        up_ref, gain_ref, shift_ref, win_ref, wout_ref, projected, *refs = refs
        sends, (field, d_lifted) = refs[:levels], refs[levels:]
        lev = place_ref[0]
        for hop in range(levels):
            start = pl.multiple_of((lev ^ hop) * channels, 8)
            for row in range(height):
                field[pl.ds(start, channels), row * width : (row + 1) * width] = convs[hop][row].astype(F32)
        convolved = field[...]
        centre = jnp.mean(convolved, axis=0, keepdims=True)
        centred = convolved - centre
        spread = jnp.mean(centred * centred, axis=0, keepdims=True)
        rstd = lax.rsqrt(spread + EPSILON)
        normed = centred * rstd
        field[...] = normed
        gain = gain_ref[...]
        lifted = (normed * gain + shift_ref[...]).astype(BF16)
        upstream = up_ref[...]
        features = wout_ref.shape[0]
        for piece in range(features // chunk):
            span = slice(piece * chunk, (piece + 1) * chunk)
            hidden = lax.dot_general(win_ref[:, span], lifted, FIRST, preferred_element_type=F32)
            d_active = jnp.dot(wout_ref[span, :], upstream, preferred_element_type=F32)
            half = 0.5 * (1.0 + lax.erf(hidden * ROOT_HALF))
            active = (hidden * half).astype(BF16)
            slope = half + hidden * jnp.exp(-0.5 * hidden * hidden) * INV_ROOT_TAU
            d_hidden = (d_active * slope).astype(BF16)
            out = lax.dot_general(wout_ref[span, :], active, FIRST, preferred_element_type=F32)
            back = jnp.dot(win_ref[:, span], d_hidden, preferred_element_type=F32)
            if piece == 0:
                projected[...] = out
                d_lifted[...] = back
            else:
                projected[...] += out
                d_lifted[...] += back
        d_normed = d_lifted[...] * gain
        normed = field[...]
        first = jnp.mean(d_normed, axis=0, keepdims=True)
        second = jnp.mean(d_normed * normed, axis=0, keepdims=True)
        field[...] = rstd * (d_normed - first - normed * second)
        for hop in range(levels):
            start = pl.multiple_of((lev ^ hop) * channels, 8)
            for row in range(height):
                sends[hop][row] = field[pl.ds(start, channels), row * width : (row + 1) * width].astype(BF16)

    return body


def finish_body(levels, channels, height, width):
    def body(place_ref, snap_ref, mask_ref, projected_ref, *refs):
        others, (result_ref, total) = refs[: levels - 1], refs[levels - 1 :]
        lev = place_ref[0]
        for hop in range(levels):
            start = pl.multiple_of((lev ^ hop) * channels, 8)
            for row in range(height):
                held = others[hop - 1][row] if hop else snap_ref[lev * height + row]
                wet = mask_ref[row : row + 1, :].astype(F32)
                value = held.astype(F32) + projected_ref[pl.ds(start, channels), row * width : (row + 1) * width]
                total[row, pl.ds(start, channels), :] = wet * value
        result_ref[...] = total[...].astype(BF16)

    return body


def gather_body(levels, channels, rows, width):
    height = rows // levels

    def body(place_ref, *refs):
        blocks, (lines_ref, off_ref, on_ref, lines) = refs[:levels], refs[levels:]
        lev, odd = place_ref[0], place_ref[1]
        for hop in range(levels):
            lines[pl.ds((lev ^ hop) * height, height)] = blocks[hop][...].astype(F32)
        lines_ref[...] = lines[...].astype(BF16)
        pack_edges(lambda row: lines[row], odd, off_ref, on_ref, rows, channels, width)

    return body


def kernel_body(levels, channels, rows, width):
    height = rows // levels

    def body(place_ref, columns_ref, *refs):
        blocks, (out_ref, grads, found_ref) = refs[:levels], refs[levels:]
        lev = place_ref[0]
        for hop in range(levels):
            grads[pl.ds((lev ^ hop) * height, height)] = blocks[hop][...].astype(F32)
        out_lane = lanes_of((8, 128))

        def step(block, carry):
            span = pl.ds(block * 8, 8)
            grad = [grads[row, span, :] for row in range(rows)]
            found = jnp.zeros((8, 128), F32)
            for col in range(TAPS):
                sums = [None] * TAPS
                for source in range(rows + REACH):
                    moved = columns_ref[col, source, span, :]
                    for a in range(TAPS):
                        row = source - a + REACH
                        if 0 <= row < rows:
                            term = grad[row] * moved
                            sums[a] = term if sums[a] is None else sums[a] + term
                for a in range(TAPS):
                    found = jnp.where(out_lane == a * TAPS + col, jnp.sum(sums[a], axis=1, keepdims=True), found)
            found_ref[span, :] = found
            return carry

        each_block(channels, step)
        out_ref[:, :channels] = found_ref[...].T[:TAP_ROWS]

    return body


def adjoint_body(levels, channels, rows, width):
    height = rows // levels

    def body(place_ref, d_ref, packs_ref, fold_ref, spread_ref, *refs):
        own_ref, others, (out_ref, lines, edges, total) = refs[0], refs[1:levels], refs[levels:]
        lev = place_ref[0]
        fill(lines, edges, lambda row: d_ref[row].astype(F32), packs_ref, fold_ref, rows, width)
        for hop in range(levels):
            taken = others[hop - 1][height:] if hop else own_ref[...]
            total[pl.ds((lev ^ hop) * height, height)] = taken.astype(F32)
        lane = lanes_of((8, width))

        def step(block, carry):
            span = pl.ds(block * 8, 8)
            sums = [None] * rows
            for col in range(TAPS):
                taps = [spread_ref[a * TAPS + col, span, :] for a in range(TAPS)]
                for source in range(rows):
                    moved = shifted(lines[source, span, :], edges[source, span, :], REACH - col, lane, width)
                    for a in range(TAPS):
                        row = source + a - REACH
                        if 0 <= row < rows:
                            term = taps[a] * moved
                            sums[row] = term if sums[row] is None else sums[row] + term
                for source in range(REACH):
                    moved = shifted(lines[rows + source, span, :], edges[rows + source, span, :], col - REACH, lane, width)
                    for depth in range(REACH - source):
                        row = rows - 1 - depth
                        sums[row] = sums[row] + taps[REACH + 1 + depth + source] * moved
            for row in range(rows):
                total[row, span, :] = total[row, span, :] + sums[row]
            return carry

        each_block(channels, step)
        out_ref[...] = total[...].astype(BF16)

    return body


def across(value, axis, target):
    count = lax.axis_size(axis)
    return lax.ppermute(value, axis, [(i, target(i) % count) for i in range(count)])


def level_swap(blocks):
    return [across(block, "lev", lambda i: i ^ hop) for hop, block in enumerate(blocks, 1)]


def edge_swap(off, on):
    return across(off, "lon", lambda i: i + 1 if i % 2 else i - 1), across(on, "lon", lambda i: i ^ 1)


def mirror(block):
    lanes = lax.axis_size("lon")
    return across(block, "lon", lambda i: lanes - 1 - i)


def sum_over_chips(terms):
    lanes = lax.axis_size("lon")
    hop = 2
    while hop < lanes:
        if 2 * hop < lanes:
            one, two, three = (across(terms, "lon", lambda i: i ^ (n * hop)) for n in (1, 2, 3))
            terms = (terms + one) + (two + three)
        else:
            terms = terms + across(terms, "lon", lambda i: i ^ hop)
        hop *= 4
    return terms


def assemble_body(levels, channels):
    def body(place_ref, *refs):
        parts, (out_ref, placed) = refs[:levels], refs[levels:]
        lev = place_ref[0]
        for hop in range(levels):
            placed[lev ^ hop] = parts[hop][...]
        for level in range(levels):
            out_ref[:, level * channels : (level + 1) * channels] = placed[level][: TAPS * TAPS, :channels]

    return body


def shards(snapshot, cotangent, ocean_mask, kernel, norm_gain, norm_shift, weight_in, weight_out):
    levels = lax.axis_size("lev")
    channels, rows, width = snapshot.shape
    height = rows // levels
    total_channels = channels * levels
    cells = height * width
    lev = lax.axis_index("lev")
    odd = lax.axis_index("lon") % 2
    place = jnp.stack([lev, odd]).astype(jnp.int32)
    groups = groups_of(rows)[0]
    weights = lax.dynamic_slice_in_dim(kernel, lev * channels, channels, 0).astype(F32)
    weights = jnp.pad(weights, ((0, 0), (0, 128 - TAPS * TAPS)))
    block = shaped(height, channels, width)
    pack = shaped(groups, channels, width)
    field = pltpu.VMEM((rows, channels, width), F32)
    deep = pltpu.VMEM((rows + REACH, channels, width), F32)
    lines = jnp.swapaxes(snapshot, 0, 1)

    packs_call = call(
        packs_body(channels, rows, width),
        [shaped(groups, channels, width, dtype=F32), shaped(*fold_shape(channels, width)[0])],
        [SMEM] + [VMEM] * 3,
        [],
        0.6,
        "packs",
    )
    off, on = call(prepare_body(channels, rows, width), [pack, pack], [SMEM, VMEM], [], 1.0, "prepare")(place, lines)
    off, on = edge_swap(off, on)
    inner, spread = call(
        inner_body(channels, rows, width),
        [shaped(rows, channels, width, dtype=F32), shaped(TAPS * TAPS, channels, width, dtype=F32)],
        [VMEM] * 2,
        [field],
        3.0,
        "inner",
    )(lines, weights)
    packs, fold = packs_call(place, lines, off, on)
    late_cotangent, _ = lax.optimization_barrier((jnp.swapaxes(cotangent, 0, 1), fold))
    upstream, up_own, *early_sends = call(
        cotangent_body(levels, channels, height, width),
        [shaped(total_channels, cells), block] + [shaped(2 * height, channels, width)] * (levels - 1),
        [SMEM] + [VMEM] * 3,
        [pltpu.VMEM((height, total_channels, width), F32)],
        1.0,
        "cotangent",
    )(place, lines, late_cotangent, ocean_mask)
    others = level_swap(early_sends)
    fold = mirror(fold)
    part = call(
        rims_body(channels, rows, width),
        shaped(rows, channels, width, dtype=F32),
        [VMEM] * 3,
        [pltpu.VMEM((groups, channels, width), F32)],
        2.0,
        "rims",
    )(inner, packs, spread)
    conv_own, *conv_sends = call(
        fold_body(levels, channels, rows, width),
        [block] * levels,
        [SMEM] + [VMEM] * 3,
        [field] + [pltpu.VMEM((REACH, channels, width), F32)] * 2,
        1.2,
        "fold",
    )(place, part, fold, spread)
    convs = [conv_own] + level_swap(conv_sends)
    convs, others = lax.optimization_barrier((convs[::-1], others))
    convs = convs[::-1]
    columns = call(
        columns_body(channels, rows, width),
        shaped(TAPS, rows + REACH, channels, width, dtype=F32),
        [VMEM] * 3,
        [deep, deep],
        2.0,
        "columns",
    )(lines, packs, fold)
    projected, d_own, *d_sends = call(
        cell_body(levels, channels, height, width, 512),
        [shaped(total_channels, cells, dtype=F32)] + [block] * levels,
        [SMEM] + [VMEM] * (levels + 5),
        [pltpu.VMEM((total_channels, cells), F32)] * 2,
        5.0,
        "cells",
    )(place, *convs, upstream, norm_gain[:, None], norm_shift[:, None], weight_in, weight_out)
    d_blocks = [d_own] + level_swap(d_sends)
    result = call(
        finish_body(levels, channels, height, width),
        shaped(height, total_channels, width),
        [SMEM] + [VMEM] * (levels + 2),
        [pltpu.VMEM((height, total_channels, width), F32)],
        1.0,
        "finish",
    )(place, lines, ocean_mask, projected, *others)
    result, d_blocks = lax.optimization_barrier((result, d_blocks[::-1]))
    d_blocks = d_blocks[::-1]
    d_lines, off, on = call(
        gather_body(levels, channels, rows, width),
        [shaped(rows, channels, width), pack, pack],
        [SMEM] + [VMEM] * levels,
        [field],
        0.8,
        "regroup",
    )(place, *d_blocks)
    columns, off = lax.optimization_barrier((columns, off))
    terms = call(
        kernel_body(levels, channels, rows, width),
        shaped(TAP_ROWS, 128, dtype=F32),
        [SMEM] + [VMEM] * (1 + levels),
        [field, pltpu.VMEM((channels, 128), F32)],
        0.01,
        "kernel_terms",
    )(place, columns, *d_blocks)
    terms = terms + across(terms, "lon", lambda i: i ^ 1)
    d_packs, d_fold = packs_call(place, d_lines, *edge_swap(off, on))
    terms, d_fold = lax.optimization_barrier((terms, d_fold))
    d_fold = mirror(d_fold)
    terms = sum_over_chips(terms)
    d_snapshot = call(
        adjoint_body(levels, channels, rows, width),
        shaped(rows, channels, width),
        [SMEM] + [VMEM] * (4 + levels),
        [deep, deep, field],
        4.0,
        "adjoint",
    )(place, d_lines, d_packs, d_fold, spread, up_own, *others)
    others = level_swap([terms] * (levels - 1))
    others, _ = lax.optimization_barrier((others, d_snapshot))
    kernel_grad = call(
        assemble_body(levels, channels),
        shaped(TAPS * TAPS, total_channels, dtype=F32),
        [SMEM] + [VMEM] * levels,
        [pltpu.VMEM((levels, TAP_ROWS, 128), F32)],
        0.8,
        "assemble",
    )(place, terms, *others)
    return (jnp.swapaxes(result, 0, 1), jnp.swapaxes(d_snapshot, 0, 1), kernel_grad.T)


def solution(mesh):
    placed = (
        P("lev", None, "lon"),
        P(None, "lev", "lon"),
        P("lev", "lon"),
        P(),
        P(),
        P(),
        P(),
        P(),
    )
    return jax.shard_map(
        shards,
        mesh=mesh,
        in_specs=placed,
        out_specs=(P(None, "lev", "lon"), P("lev", None, "lon"), P()),
        check_vma=False,
    )
```

```python
import jax
import jax.numpy as jnp
from jax import lax
from jax.experimental import pallas as pl
from jax.experimental.pallas import tpu as pltpu
from jax.sharding import PartitionSpec as P

TAPS = 7
REACH = TAPS // 2
EPSILON = 1e-06
ROOT_HALF = 0.7071067811865476
INV_ROOT_TAU = 0.3989422804014327
F32 = jnp.float32
BF16 = jnp.bfloat16
VMEM = pl.BlockSpec(memory_space=pltpu.VMEM)
SMEM = pl.BlockSpec(memory_space=pltpu.SMEM)
SPAN = 2 * REACH
TAP_ROWS = (TAPS * TAPS + 7) // 8 * 8
FIRST = (((0,), (0,)), ((), ()))
LIMIT = 24 * 1024 * 1024


def call(body, out, specs, scratch, micros, name):
    return pl.pallas_call(
        body,
        out_shape=out,
        in_specs=specs,
        out_specs=jax.tree.map(lambda _: VMEM, out),
        scratch_shapes=scratch,
        compiler_params=pltpu.CompilerParams(vmem_limit_bytes=LIMIT),
        cost_estimate=pl.CostEstimate(flops=int(micros * 1.1e9), bytes_accessed=0, transcendentals=0),
        name=name,
    )


def shaped(*shape, dtype=BF16):
    return jax.ShapeDtypeStruct(shape, dtype)


def lanes_of(shape):
    return lax.broadcasted_iota(jnp.int32, shape, len(shape) - 1)


def groups_of(rows):
    per = rows
    while (per + 2 * REACH) * SPAN > 128 or rows % per:
        per -= 1
    return rows // per, per


def ones_where(mask):
    return jnp.where(mask, 1.0, 0.0)


def right_lanes(lane, per, width):
    low = (per + REACH) * SPAN - REACH
    base = SPAN * ((width + SPAN - 1) // SPAN) - width
    place = jnp.where(lane >= low, lane + base, lane)
    return place - SPAN * ((place * 171) >> 10) < REACH


def pack_edges(read, odd, off_ref, on_ref, rows, channels, width):
    count, per = groups_of(rows)
    lane = lanes_of((1, width))
    turn = odd.astype(F32)
    for group in range(count):
        off = jnp.zeros((channels, width), F32)
        on = jnp.zeros((channels, width), F32)
        for place in range(per):
            base = SPAN * place
            line = pltpu.roll(read(group * per + place), base, 1) if place else read(group * per)
            first = ones_where((lane >= base) & (lane < base + REACH))
            spot = (base - REACH) % width
            last = ones_where((lane >= spot) & (lane < spot + REACH))
            off = off + line * (first + turn * (last - first))
            on = on + line * (last + turn * (first - last))
        off_ref[group] = off.astype(BF16)
        on_ref[group] = on.astype(BF16)


def flip_lanes(value, width, top):
    row = lax.broadcasted_iota(jnp.int32, (width, width), 0)
    col = lax.broadcasted_iota(jnp.int32, (width, width), 1)
    exchange = ((row + col == top % width) | (row + col == top % width + width)).astype(BF16)
    return jnp.dot(value, exchange, preferred_element_type=F32)


def fold_shape(channels, width):
    parts = 4 if channels % 32 == 0 else 1
    share = channels // parts
    head = (share + 15) // 16 * 16 if parts > 1 else channels
    return ((head + REACH * channels, width) if parts > 1 else (REACH + 1, channels, width)), head, parts


def fold_lanes(per, width):
    lane = lanes_of((1, width))
    begin = SPAN * (per - REACH) - REACH
    return begin, ones_where((lane >= begin) & (lane < SPAN * per - REACH))


def write_fold(fold_ref, value, lines_ref, channels, per, width):
    _, head, parts = fold_shape(channels, width)
    if parts == 1:
        fold_ref[0:REACH] = lines_ref[...]
        fold_ref[REACH] = value.astype(BF16)
        return
    begin, ends = fold_lanes(per, width)
    share = channels // parts
    kept = value * ends
    packed = jnp.zeros((share, width), F32)
    for part in range(parts):
        packed = packed + pltpu.roll(kept[part * share : (part + 1) * share], (part * (width // parts) - begin) % width, 1)
    if head > share:
        packed = jnp.concatenate([packed, jnp.zeros((head - share, width), F32)], axis=0)
    fold_ref[0:head, :] = packed.astype(BF16)
    for row in range(REACH):
        fold_ref[head + row * channels : head + (row + 1) * channels, :] = lines_ref[row]


def flip_fold(lines_of, fold_ref, channels, per, width):
    _, head, parts = fold_shape(channels, width)
    begin, ends = fold_lanes(per, width)
    if parts == 1:
        packed = fold_ref[REACH].astype(F32)
        for depth in range(REACH):
            lines_of[depth] = flip_lanes(fold_ref[REACH - 1 - depth], width, width - 1)
    else:
        held = fold_ref[0:head, :].astype(F32)[: channels // parts]
        pieces = [pltpu.roll(held, (begin - part * (width // parts)) % width, 1) for part in range(parts)]
        packed = jnp.concatenate(pieces, axis=0)
        flipped = flip_lanes(fold_ref[head : head + REACH * channels, :], width, width - 1)
        for depth in range(REACH):
            row = REACH - 1 - depth
            lines_of[depth] = flipped[row * channels : (row + 1) * channels]
    return flip_lanes((packed * ends).astype(BF16), width, 2 * SPAN * per - SPAN - 1)


def each_block(channels, step, most=4):
    blocks = channels // 8
    unroll = max(n for n in range(1, most + 1) if blocks % n == 0)
    lax.fori_loop(0, blocks, step, 0, unroll=unroll)


def unpack(group, place, width):
    shift = (-SPAN * place) % width
    return pltpu.roll(group, shift, 1) if shift else group


def fill(lines, edges, read, packs_ref, fold_ref, rows, width):
    per = groups_of(rows)[1]
    folded = flip_fold(lines.at[pl.ds(rows, REACH)], fold_ref, lines.shape[1], per, width)
    for row in range(rows):
        lines[row] = read(row)
        edges[row] = unpack(packs_ref[row // per], row % per, width)
    for depth in range(REACH):
        edges[rows + depth] = unpack(folded, per + depth, width)


def shifted(line, edge, step, lane, width):
    if step == 0:
        return line
    if step > 0:
        return pltpu.roll(jnp.where(lane < step, edge, line), width - step, 1)
    return pltpu.roll(jnp.where(lane >= width + step, edge, line), -step, 1)


def prepare_body(channels, rows, width):
    def body(place_ref, snap_ref, off_ref, on_ref):
        pack_edges(lambda row: snap_ref[row].astype(F32), place_ref[1], off_ref, on_ref, rows, channels, width)

    return body


def packs_body(channels, rows, width):
    count, per = groups_of(rows)

    def body(place_ref, lines_ref, off_ref, on_ref, packs_ref, fold_ref):
        lane = lanes_of((1, width))
        right = ones_where(right_lanes(lane, per, width))
        near = right + place_ref[1].astype(F32) * (1.0 - 2.0 * right)
        far = 1.0 - near
        for group in range(count):
            value = on_ref[group].astype(F32) * near + off_ref[group].astype(F32) * far
            packs_ref[group] = value
        write_fold(fold_ref, value, lines_ref.at[pl.ds(rows - REACH, REACH)], channels, per, width)

    return body


def inner_body(channels, rows, width):
    def body(snap_ref, weight_ref, out_ref, spread_ref, lines):
        lines[...] = snap_ref[...].astype(F32)
        weights = weight_ref[...].astype(BF16)
        row = lax.broadcasted_iota(jnp.int32, (128, 2 * width), 0)
        second = jnp.where(lax.broadcasted_iota(jnp.int32, (128, 2 * width), 1) < width, 0, 1)
        for tap in range(0, TAPS * TAPS, 2):
            pick = jnp.where(row == second + tap, 1.0, 0.0).astype(BF16)
            pair = jnp.dot(weights, pick, preferred_element_type=F32)
            spread_ref[tap] = pair[:, :width]
            if tap + 1 < TAPS * TAPS:
                spread_ref[tap + 1] = pair[:, width:]
        lane = lanes_of((8, width))

        def step(block, carry):
            span = pl.ds(block * 8, 8)
            sums = [None] * rows
            for col in range(TAPS):
                taps = [spread_ref[a * TAPS + col, span, :] for a in range(TAPS)]
                for source in range(rows):
                    moved = shifted(lines[source, span, :], 0.0, col - REACH, lane, width)
                    for a in range(TAPS):
                        row = source - a + REACH
                        if 0 <= row < rows:
                            term = taps[a] * moved
                            sums[row] = term if sums[row] is None else sums[row] + term
            for row in range(rows):
                out_ref[row, span, :] = sums[row]
            return carry

        each_block(channels, step)

    return body


def rims_body(channels, rows, width):
    count, per = groups_of(rows)

    def body(inner_ref, packs_ref, spread_ref, out_ref, packed):
        wide = lanes_of((1, width))
        tail = ones_where((wide >= SPAN * (per - REACH) - REACH) & (wide < SPAN * per - REACH))
        begin = ones_where((wide < SPAN * REACH - REACH) | (wide >= width - REACH))
        for group in range(count):
            value = packs_ref[group]
            if group:
                value = value + pltpu.roll(packs_ref[group - 1] * tail, (-SPAN * per) % width, 1)
            if group + 1 < count:
                value = value + pltpu.roll(packs_ref[group + 1] * begin, SPAN * per, 1)
            packed[group] = value
        lane = lanes_of((8, width))
        right = right_lanes(lane, per, width)
        rim = (lane < REACH) | (lane >= width - REACH)

        def step(block, carry):
            span = pl.ds(block * 8, 8)
            for group in range(count):
                near = packed[group, span, :]
                from_right = jnp.where(right, near, 0.0)
                from_left = jnp.where(right, 0.0, near)
                sums = [None, None]
                for a in range(TAPS):
                    for col in range(TAPS):
                        if col == REACH:
                            continue
                        side = col > REACH
                        move = (-(SPAN * (a - REACH) + col - REACH)) % width
                        term = spread_ref[a * TAPS + col, span, :] * pltpu.roll(from_right if side else from_left, move, 1)
                        sums[side] = term if sums[side] is None else sums[side] + term
                rims = jnp.where(right, sums[0], sums[1])
                for place in range(per):
                    row = group * per + place
                    out_ref[row, span, :] = inner_ref[row, span, :] + jnp.where(rim, unpack(rims, place, width), 0.0)
            return carry

        each_block(channels, step)

    return body


def fold_body(levels, channels, rows, width):
    height = rows // levels
    per = groups_of(rows)[1]

    def body(place_ref, part_ref, fold_ref, spread_ref, *rest):
        sends, (total, lines, edges) = rest[:levels], rest[levels:]
        lev = place_ref[0]
        folded = flip_fold(lines, fold_ref, channels, per, width)
        for depth in range(REACH):
            edges[depth] = unpack(folded, per + depth, width)
        lane = lanes_of((8, width))

        def step(block, carry):
            span = pl.ds(block * 8, 8)
            sums = [part_ref[rows - 1 - up, span, :] for up in range(REACH)]
            for depth in range(REACH):
                for col in range(TAPS):
                    moved = shifted(lines[depth, span, :], edges[depth, span, :], col - REACH, lane, width)
                    for up in range(REACH - depth):
                        a = REACH + 1 + depth + up
                        sums[up] = sums[up] + spread_ref[a * TAPS + col, span, :] * moved
            for up in range(REACH):
                total[rows - 1 - up, span, :] = sums[up]
            return carry

        each_block(channels, step, 12)
        total[0 : rows - REACH] = part_ref[0 : rows - REACH]
        for hop in range(levels):
            sends[hop][...] = total[pl.ds((lev ^ hop) * height, height)].astype(BF16)

    return body


def columns_body(channels, rows, width):
    def body(snap_ref, packs_ref, fold_ref, out_ref, lines, edges):
        fill(lines, edges, lambda row: snap_ref[row].astype(F32), packs_ref, fold_ref, rows, width)
        lane = lanes_of((channels, width))
        for col in range(TAPS):
            for source in range(rows + REACH):
                out_ref[col, source] = shifted(lines[source], edges[source], col - REACH, lane, width)

    return body


def cotangent_body(levels, channels, height, width):
    def body(place_ref, snap_ref, cot_ref, mask_ref, up_ref, own_ref, *rest):
        sends, lines = rest[: levels - 1], rest[levels - 1]
        lev = place_ref[0]
        wet = mask_ref[...].astype(F32)
        lines[...] = cot_ref[...].astype(F32) * wet[:, None, :]
        for row in range(height):
            up_ref[:, row * width : (row + 1) * width] = lines[row].astype(BF16)
        for hop in range(levels):
            start = pl.multiple_of((lev ^ hop) * channels, 8)
            for row in range(height):
                value = lines[row, pl.ds(start, channels), :].astype(BF16)
                if hop:
                    sends[hop - 1][height + row] = value
                else:
                    own_ref[row] = value
            if hop:
                sends[hop - 1][0:height] = snap_ref[pl.ds((lev ^ hop) * height, height)]

    return body


def cell_body(levels, channels, height, width, chunk):
    def body(place_ref, *refs):
        convs, refs = refs[:levels], refs[levels:]
        up_ref, gain_ref, shift_ref, win_ref, wout_ref, projected, *refs = refs
        sends, (field, d_lifted) = refs[:levels], refs[levels:]
        lev = place_ref[0]
        for hop in range(levels):
            start = pl.multiple_of((lev ^ hop) * channels, 8)
            for row in range(height):
                field[pl.ds(start, channels), row * width : (row + 1) * width] = convs[hop][row].astype(F32)
        convolved = field[...]
        centre = jnp.mean(convolved, axis=0, keepdims=True)
        centred = convolved - centre
        spread = jnp.mean(centred * centred, axis=0, keepdims=True)
        rstd = lax.rsqrt(spread + EPSILON)
        normed = centred * rstd
        field[...] = normed
        gain = gain_ref[...]
        lifted = (normed * gain + shift_ref[...]).astype(BF16)
        upstream = up_ref[...]
        features = wout_ref.shape[0]
        for piece in range(features // chunk):
            span = slice(piece * chunk, (piece + 1) * chunk)
            hidden = lax.dot_general(win_ref[:, span], lifted, FIRST, preferred_element_type=F32)
            d_active = jnp.dot(wout_ref[span, :], upstream, preferred_element_type=F32)
            half = 0.5 * (1.0 + lax.erf(hidden * ROOT_HALF))
            active = (hidden * half).astype(BF16)
            slope = half + hidden * jnp.exp(-0.5 * hidden * hidden) * INV_ROOT_TAU
            d_hidden = (d_active * slope).astype(BF16)
            out = lax.dot_general(wout_ref[span, :], active, FIRST, preferred_element_type=F32)
            back = jnp.dot(win_ref[:, span], d_hidden, preferred_element_type=F32)
            if piece == 0:
                projected[...] = out
                d_lifted[...] = back
            else:
                projected[...] += out
                d_lifted[...] += back
        d_normed = d_lifted[...] * gain
        normed = field[...]
        first = jnp.mean(d_normed, axis=0, keepdims=True)
        second = jnp.mean(d_normed * normed, axis=0, keepdims=True)
        field[...] = rstd * (d_normed - first - normed * second)
        for hop in range(levels):
            start = pl.multiple_of((lev ^ hop) * channels, 8)
            for row in range(height):
                sends[hop][row] = field[pl.ds(start, channels), row * width : (row + 1) * width].astype(BF16)

    return body


def finish_body(levels, channels, height, width):
    def body(place_ref, snap_ref, mask_ref, projected_ref, *refs):
        others, (result_ref, total) = refs[: levels - 1], refs[levels - 1 :]
        lev = place_ref[0]
        for hop in range(levels):
            start = pl.multiple_of((lev ^ hop) * channels, 8)
            for row in range(height):
                held = others[hop - 1][row] if hop else snap_ref[lev * height + row]
                wet = mask_ref[row : row + 1, :].astype(F32)
                value = held.astype(F32) + projected_ref[pl.ds(start, channels), row * width : (row + 1) * width]
                total[row, pl.ds(start, channels), :] = wet * value
        result_ref[...] = total[...].astype(BF16)

    return body


def gather_body(levels, channels, rows, width):
    height = rows // levels

    def body(place_ref, *refs):
        blocks, (lines_ref, off_ref, on_ref, lines) = refs[:levels], refs[levels:]
        lev, odd = place_ref[0], place_ref[1]
        for hop in range(levels):
            lines[pl.ds((lev ^ hop) * height, height)] = blocks[hop][...].astype(F32)
        lines_ref[...] = lines[...].astype(BF16)
        pack_edges(lambda row: lines[row], odd, off_ref, on_ref, rows, channels, width)

    return body


def kernel_body(levels, channels, rows, width):
    height = rows // levels

    def body(place_ref, columns_ref, *refs):
        blocks, (out_ref, grads, found_ref) = refs[:levels], refs[levels:]
        lev = place_ref[0]
        for hop in range(levels):
            grads[pl.ds((lev ^ hop) * height, height)] = blocks[hop][...].astype(F32)
        out_lane = lanes_of((8, 128))

        def step(block, carry):
            span = pl.ds(block * 8, 8)
            grad = [grads[row, span, :] for row in range(rows)]
            found = jnp.zeros((8, 128), F32)
            for col in range(TAPS):
                sums = [None] * TAPS
                for source in range(rows + REACH):
                    moved = columns_ref[col, source, span, :]
                    for a in range(TAPS):
                        row = source - a + REACH
                        if 0 <= row < rows:
                            term = grad[row] * moved
                            sums[a] = term if sums[a] is None else sums[a] + term
                for a in range(TAPS):
                    found = jnp.where(out_lane == a * TAPS + col, jnp.sum(sums[a], axis=1, keepdims=True), found)
            found_ref[span, :] = found
            return carry

        each_block(channels, step)
        out_ref[:, :channels] = found_ref[...].T[:TAP_ROWS]

    return body


def adjoint_body(levels, channels, rows, width):
    height = rows // levels

    def body(place_ref, d_ref, packs_ref, fold_ref, spread_ref, *refs):
        own_ref, others, (out_ref, lines, edges, total) = refs[0], refs[1:levels], refs[levels:]
        lev = place_ref[0]
        fill(lines, edges, lambda row: d_ref[row].astype(F32), packs_ref, fold_ref, rows, width)
        for hop in range(levels):
            taken = others[hop - 1][height:] if hop else own_ref[...]
            total[pl.ds((lev ^ hop) * height, height)] = taken.astype(F32)
        lane = lanes_of((8, width))

        def step(block, carry):
            span = pl.ds(block * 8, 8)
            sums = [None] * rows
            for col in range(TAPS):
                taps = [spread_ref[a * TAPS + col, span, :] for a in range(TAPS)]
                for source in range(rows):
                    moved = shifted(lines[source, span, :], edges[source, span, :], REACH - col, lane, width)
                    for a in range(TAPS):
                        row = source + a - REACH
                        if 0 <= row < rows:
                            term = taps[a] * moved
                            sums[row] = term if sums[row] is None else sums[row] + term
                for source in range(REACH):
                    moved = shifted(lines[rows + source, span, :], edges[rows + source, span, :], col - REACH, lane, width)
                    for depth in range(REACH - source):
                        row = rows - 1 - depth
                        sums[row] = sums[row] + taps[REACH + 1 + depth + source] * moved
            for row in range(rows):
                total[row, span, :] = total[row, span, :] + sums[row]
            return carry

        each_block(channels, step, 12)
        out_ref[...] = total[...].astype(BF16)

    return body


def across(value, axis, target):
    count = lax.axis_size(axis)
    return lax.ppermute(value, axis, [(i, target(i) % count) for i in range(count)])


def level_swap(blocks):
    return [across(block, "lev", lambda i: i ^ hop) for hop, block in enumerate(blocks, 1)]


def edge_swap(off, on):
    return across(off, "lon", lambda i: i + 1 if i % 2 else i - 1), across(on, "lon", lambda i: i ^ 1)


def mirror(block):
    lanes = lax.axis_size("lon")
    return across(block, "lon", lambda i: lanes - 1 - i)


def sum_over_chips(terms):
    lanes = lax.axis_size("lon")
    hop = 2
    while hop < lanes:
        if 2 * hop < lanes:
            one, two, three = (across(terms, "lon", lambda i: i ^ (n * hop)) for n in (1, 2, 3))
            terms = (terms + one) + (two + three)
        else:
            terms = terms + across(terms, "lon", lambda i: i ^ hop)
        hop *= 4
    return terms


def assemble_body(levels, channels):
    def body(place_ref, *refs):
        parts, out_ref = refs[:levels], refs[levels]
        placed = {}
        lev = place_ref[0]
        for hop in range(levels):
            value = parts[hop][...]
            for level in range(levels):
                placed[level] = value if hop == 0 else jnp.where(lev ^ hop == level, value, placed[level])
        for level in range(levels):
            out_ref[:, level * channels : (level + 1) * channels] = placed[level][: TAPS * TAPS, :channels]

    return body


def shards(snapshot, cotangent, ocean_mask, kernel, norm_gain, norm_shift, weight_in, weight_out):
    levels = lax.axis_size("lev")
    channels, rows, width = snapshot.shape
    height = rows // levels
    total_channels = channels * levels
    cells = height * width
    lev = lax.axis_index("lev")
    odd = lax.axis_index("lon") % 2
    place = jnp.stack([lev, odd]).astype(jnp.int32)
    groups = groups_of(rows)[0]
    weights = lax.dynamic_slice_in_dim(kernel, lev * channels, channels, 0).astype(F32)
    weights = jnp.pad(weights, ((0, 0), (0, 128 - TAPS * TAPS)))
    block = shaped(height, channels, width)
    pack = shaped(groups, channels, width)
    field = pltpu.VMEM((rows, channels, width), F32)
    deep = pltpu.VMEM((rows + REACH, channels, width), F32)
    lines = jnp.swapaxes(snapshot, 0, 1)

    packs_call = call(
        packs_body(channels, rows, width),
        [shaped(groups, channels, width, dtype=F32), shaped(*fold_shape(channels, width)[0])],
        [SMEM] + [VMEM] * 3,
        [],
        0.6,
        "packs",
    )
    off, on = call(prepare_body(channels, rows, width), [pack, pack], [SMEM, VMEM], [], 1.0, "prepare")(place, lines)
    off, on = edge_swap(off, on)
    inner, spread = call(
        inner_body(channels, rows, width),
        [shaped(rows, channels, width, dtype=F32), shaped(TAPS * TAPS, channels, width, dtype=F32)],
        [VMEM] * 2,
        [field],
        3.0,
        "inner",
    )(lines, weights)
    packs, fold = packs_call(place, lines, off, on)
    late_cotangent, _ = lax.optimization_barrier((jnp.swapaxes(cotangent, 0, 1), fold))
    upstream, up_own, *early_sends = call(
        cotangent_body(levels, channels, height, width),
        [shaped(total_channels, cells), block] + [shaped(2 * height, channels, width)] * (levels - 1),
        [SMEM] + [VMEM] * 3,
        [pltpu.VMEM((height, total_channels, width), F32)],
        1.0,
        "cotangent",
    )(place, lines, late_cotangent, ocean_mask)
    others = level_swap(early_sends)
    fold = mirror(fold)
    part = call(
        rims_body(channels, rows, width),
        shaped(rows, channels, width, dtype=F32),
        [VMEM] * 3,
        [pltpu.VMEM((groups, channels, width), F32)],
        2.0,
        "rims",
    )(inner, packs, spread)
    conv_own, *conv_sends = call(
        fold_body(levels, channels, rows, width),
        [block] * levels,
        [SMEM] + [VMEM] * 3,
        [field] + [pltpu.VMEM((REACH, channels, width), F32)] * 2,
        1.2,
        "fold",
    )(place, part, fold, spread)
    convs = [conv_own] + level_swap(conv_sends)
    convs, others = lax.optimization_barrier((convs[::-1], others))
    convs = convs[::-1]
    columns = call(
        columns_body(channels, rows, width),
        shaped(TAPS, rows + REACH, channels, width, dtype=F32),
        [VMEM] * 3,
        [deep, deep],
        2.0,
        "columns",
    )(lines, packs, fold)
    projected, d_own, *d_sends = call(
        cell_body(levels, channels, height, width, 512),
        [shaped(total_channels, cells, dtype=F32)] + [block] * levels,
        [SMEM] + [VMEM] * (levels + 5),
        [pltpu.VMEM((total_channels, cells), F32)] * 2,
        5.0,
        "cells",
    )(place, *convs, upstream, norm_gain[:, None], norm_shift[:, None], weight_in, weight_out)
    d_blocks = [d_own] + level_swap(d_sends)
    result = call(
        finish_body(levels, channels, height, width),
        shaped(height, total_channels, width),
        [SMEM] + [VMEM] * (levels + 2),
        [pltpu.VMEM((height, total_channels, width), F32)],
        1.0,
        "finish",
    )(place, lines, ocean_mask, projected, *others)
    result, d_blocks = lax.optimization_barrier((result, d_blocks[::-1]))
    d_blocks = d_blocks[::-1]
    d_lines, off, on = call(
        gather_body(levels, channels, rows, width),
        [shaped(rows, channels, width), pack, pack],
        [SMEM] + [VMEM] * levels,
        [field],
        0.8,
        "regroup",
    )(place, *d_blocks)
    columns, off = lax.optimization_barrier((columns, off))
    terms = call(
        kernel_body(levels, channels, rows, width),
        shaped(TAP_ROWS, 128, dtype=F32),
        [SMEM] + [VMEM] * (1 + levels),
        [field, pltpu.VMEM((channels, 128), F32)],
        0.01,
        "kernel_terms",
    )(place, columns, *d_blocks)
    terms = terms + across(terms, "lon", lambda i: i ^ 1)
    d_packs, d_fold = packs_call(place, d_lines, *edge_swap(off, on))
    terms, d_fold = lax.optimization_barrier((terms, d_fold))
    d_fold = mirror(d_fold)
    terms = sum_over_chips(terms)
    d_snapshot = call(
        adjoint_body(levels, channels, rows, width),
        shaped(rows, channels, width),
        [SMEM] + [VMEM] * (4 + levels),
        [deep, deep, field],
        4.0,
        "adjoint",
    )(place, d_lines, d_packs, d_fold, spread, up_own, *others)
    others = level_swap([terms] * (levels - 1))
    others, _ = lax.optimization_barrier((others, d_snapshot))
    kernel_grad = call(
        assemble_body(levels, channels),
        shaped(TAPS * TAPS, total_channels, dtype=F32),
        [SMEM] + [VMEM] * levels,
        [],
        0.8,
        "assemble",
    )(place, terms, *others)
    return (jnp.swapaxes(result, 0, 1), jnp.swapaxes(d_snapshot, 0, 1), kernel_grad.T)


def solution(mesh):
    placed = (
        P("lev", None, "lon"),
        P(None, "lev", "lon"),
        P("lev", "lon"),
        P(),
        P(),
        P(),
        P(),
        P(),
    )
    return jax.shard_map(
        shards,
        mesh=mesh,
        in_specs=placed,
        out_specs=(P(None, "lev", "lon"), P("lev", None, "lon"), P()),
        check_vma=False,
    )
```
